32 devices in a mesh: seq: 16 (over z, y, x), head: 2 (over core).
Axes of the slice: x: 2, y: 2, z: 4, core: 2. Of those that a mesh axis runs over, the one named last changes fastest.
Arguments:
- hidden: float32 [2, 4096, 1536], P(None, 'seq'), may hold values from -6 to 6
- norm_gain: float32 [1536], replicated, may hold values from 0.5 to 1.5
- gate_weight: float32 [1536, 3072], P('seq', 'head'), may hold values from -0.15625 to 0.15625
- inner_weight: float32 [1536, 3072], P('seq', 'head'), may hold values from -0.15625 to 0.15625
- state_weight: float32 [1536, 256], P('seq'), may hold values from -0.15625 to 0.15625
- step_weight: float32 [1536, 48], P('seq', 'head'), may hold values from -0.15625 to 0.15625
- conv_weight: float32 [4, 3072], P(None, 'head'), may hold values from -3 to 3
- conv_bias: float32 [3072], P('head'), may hold values from -0.5 to 0.5
- state_conv_weight: float32 [4, 256], replicated, may hold values from -3 to 3
- state_conv_bias: float32 [256], replicated, may hold values from -0.5 to 0.5
- step_bias: float32 [48], P('head'), may hold values from -9.5 to -8.5
- log_rate: float32 [48], P('head'), may hold values from -3 to 5.5
- skip_gain: float32 [48], P('head'), may hold values from 0.5 to 1.5
- out_gain: float32 [3072], P('head'), may hold values from 0.5 to 1.5
- output_projection_weight: float32 [1536, 3072], P('seq', 'head'), may hold values from -0.109375 to 0.109375
- cotangent: float32 [2, 4096, 1536], P(None, 'seq'), may hold values from -6 to 6
Outputs:
- output: float32 [2, 4096, 1536], P(None, 'seq')
- hidden_grad: float32 [2, 4096, 1536], P(None, 'seq')
- norm_gain_grad: float32 [1536], replicated
- gate_weight_grad: float32 [1536, 3072], P('seq', 'head')
- inner_weight_grad: float32 [1536, 3072], P('seq', 'head')
- state_weight_grad: float32 [1536, 256], P('seq')
- step_weight_grad: float32 [1536, 48], P('seq', 'head')
- conv_weight_grad: float32 [4, 3072], P(None, 'head')
- conv_bias_grad: float32 [3072], P('head')
- state_conv_weight_grad: float32 [4, 256], replicated
- memory_filter_offset_derivative: float32 [256], replicated
- step_bias_grad: float32 [48], P('head')
- log_rate_grad: float32 [48], P('head')
- skip_gain_grad: float32 [48], P('head')
- out_gain_grad: float32 [3072], P('head')
- out_weight_grad: float32 [1536, 3072], P('seq', 'head')
The draws below stay inside these ranges and needn't reach their ends.
All inputs are finite; a program needn't handle non-finite values.
Results may differ from the reference program's by a relative error of at most 0.005.
The reference program's roundings to bfloat16 on the way count: a program that leaves them out, or rounds other values in their place, can miss the bound.
Values may be sent and summed in bfloat16 or wider, within the bound.
No kernel may reach another device: no remote copies, remote signals or barrier semaphores. Data moves between devices by JAX's collectives and lax.ppermute only.
A program may use at most 256 MiB of HBM per device.

```python
from functools import partial
import jax
import jax.numpy as jnp
from jax import lax

D = 1536
HEADS = 48
HEADDIM = 64
STATE = 128
CONV = 4
GROUP = 256
SEQS = 2
INNER = 3072
LENGTH = 4096


def block_scale(own_key, dims, shards, smallest, top_value):
    loudness = 1.0
    for dim, shards_of in shards:
        draws = jax.random.uniform(jax.random.fold_in(jax.random.fold_in(own_key, 6), dim), (shards_of,), jnp.float32, smallest / len(shards), top_value / len(shards))
        loudness = loudness * jnp.repeat(jnp.exp(draws), dims[dim] // shards_of).reshape((-1,) + (1,) * (len(dims) - 1 - dim))
    return loudness


def gaussian(own_key, shape, deviation, most, split=(), dtype=jnp.bfloat16):
    array = jax.random.normal(own_key, shape, jnp.float32) * deviation
    if len(split) > 0:
        array = block_scale(own_key, shape, split, -0.22, 0.18) * array
    return jnp.clip(array, min=-most, max=most).astype(dtype)


def setup_inputs(seed: int = 0) -> dict:
    key_of = jax.random.split(jax.random.key(seed), 17)
    hidden = gaussian(key_of[0], (SEQS, LENGTH, D), 1.0, 6.0, ((1, 16),), jnp.float32)
    norm_gain = jnp.clip(1.0 + 0.1 * jax.random.normal(key_of[1], (D,), jnp.float32), 0.5, 1.5)
    gate_weight = gaussian(key_of[2], (D, INNER), D ** -0.5, 0.15625, ((0, 16), (1, 2)), jnp.float32)
    inner_weight = gaussian(key_of[3], (D, INNER), D ** -0.5, 0.15625, ((0, 16), (1, 2)), jnp.float32)
    state_weight = gaussian(key_of[4], (D, 2 * STATE), D ** -0.5, 0.15625, ((0, 16),), jnp.float32)
    step_weight = gaussian(key_of[5], (D, HEADS), D ** -0.5, 0.15625, ((0, 16), (1, 2)), jnp.float32)
    conv_weight = gaussian(key_of[6], (CONV, INNER), CONV ** -0.5, 3.0, ((1, 2),), jnp.float32)
    conv_bias = jnp.clip(jax.random.uniform(key_of[7], (INNER,), jnp.float32, -0.5, 0.5) * block_scale(key_of[7], (INNER,), ((0, 2),), -0.4, 0.0), -0.5, 0.5)
    state_conv_weight = gaussian(key_of[8], (CONV, 2 * STATE), CONV ** -0.5, 3.0, (), jnp.float32)
    state_conv_bias = jnp.clip(jax.random.uniform(key_of[9], (2 * STATE,), jnp.float32, -0.5, 0.5), -0.5, 0.5)
    step_bias = jnp.clip(-9.5 + 1.0 * jax.random.uniform(key_of[10], (HEADS,), jnp.float32) ** block_scale(key_of[10], (HEADS,), ((0, 2),), -0.2, 0.2), -9.5, -8.5)
    log_rate = jnp.clip(-3.0 + 8.5 * jax.random.uniform(key_of[11], (HEADS,), jnp.float32) ** block_scale(key_of[11], (HEADS,), ((0, 2),), -0.2, 0.2), -3.0, 5.5)
    skip_gain = jnp.clip(0.5 + 1.0 * jax.random.uniform(key_of[12], (HEADS,), jnp.float32) ** block_scale(key_of[12], (HEADS,), ((0, 2),), -0.2, 0.2), 0.5, 1.5)
    out_gain = jnp.clip(1.0 + 0.1 * jax.random.normal(key_of[13], (INNER,), jnp.float32), 0.5, 1.5)
    output_projection_weight = gaussian(key_of[14], (D, INNER), INNER ** -0.5, 0.109375, ((0, 16), (1, 2)), jnp.float32)
    cotangent = gaussian(key_of[15], (SEQS, LENGTH, D), 1.0, 6.0, ((1, 16),), jnp.float32)
    return dict(hidden=hidden, norm_gain=norm_gain, gate_weight=gate_weight, inner_weight=inner_weight, state_weight=state_weight, step_weight=step_weight, conv_weight=conv_weight, conv_bias=conv_bias, state_conv_weight=state_conv_weight, state_conv_bias=state_conv_bias, step_bias=step_bias, log_rate=log_rate, skip_gain=skip_gain, out_gain=out_gain, output_projection_weight=output_projection_weight, cotangent=cotangent)


EPS = 1e-05
FINE_ARITHMETIC = lax.Precision.HIGHEST

@jax.custom_vjp
def lowered_copy(v):
    return lax.optimization_barrier(v.astype(jnp.bfloat16)).astype(jnp.float32)

@jax.custom_vjp
def lowered_backward(v):
    return v

def low_keep(v):
    return (lowered_copy(v), None)

def low_pass(kept, grad):
    return (grad,)

def back_keep(v):
    return (v, None)

def back_low(kept, grad):
    return (lowered_copy(grad),)
lowered_copy.defvjp(low_keep, low_pass)
lowered_backward.defvjp(back_keep, back_low)

def project(rescaled_activations, coefficient_table):
    return jnp.einsum('heu,uk->hek', rescaled_activations, coefficient_table, precision=FINE_ARITHMETIC)

def group_step(decay_rate, skip_gain, incoming, pieces):
    inputs_x, write_in, read_in, step_size = pieces
    length_q = step_size.shape[2]
    cumulative = jnp.cumsum(step_size * decay_rate[None, :, None], axis=2)
    low_x = lowered_copy(inputs_x)
    low_write = lowered_copy(write_in)
    low_read = lowered_copy(read_in)
    scores = lowered_backward(jnp.einsum('stn,sun->stu', low_read, low_write, precision=FINE_ARITHMETIC))
    row_index = jnp.arange(length_q)
    lower = row_index[:, None] >= row_index[None, :]
    decay_table = jnp.exp(jnp.where(lower, cumulative[:, :, :, None] - cumulative[:, :, None, :], -1e+30))
    weights = lowered_copy(scores[:, None] * decay_table * step_size[:, :, None, :])
    diagonal = jnp.einsum('shtu,suhp->sthp', weights, low_x, precision=FINE_ARITHMETIC)
    tail_weight = jnp.exp(cumulative[:, :, -1:] - cumulative) * step_size
    write_scaled = lowered_copy(write_in[:, None] * tail_weight[..., None])
    group_state = lowered_backward(jnp.einsum('shqn,sqhp->shnp', write_scaled, low_x, precision=FINE_ARITHMETIC))
    read_scaled = lowered_copy(read_in[:, None] * jnp.exp(cumulative)[..., None])
    offdiag = jnp.einsum('shqn,shnp->sqhp', read_scaled, lowered_copy(incoming), precision=FINE_ARITHMETIC)
    mixer = lowered_backward(diagonal + offdiag) + skip_gain[:, None] * inputs_x
    outgoing = jnp.exp(cumulative[:, :, -1])[..., None, None] * incoming + group_state
    return (outgoing, mixer)

def forward(hidden, norm_gain, gate_weight, inner_weight, state_weight, step_weight, conv_weight, conv_bias, state_conv_weight, state_conv_bias, step_bias, log_rate, skip_gain, out_gain, output_projection_weight):
    num_seqs, length_l, model_width = hidden.shape
    inv_rms = lax.rsqrt(lax.optimization_barrier(jnp.mean(hidden * hidden, axis=-1, keepdims=True)) + EPS)
    rescaled_activations = lowered_copy(hidden * inv_rms * norm_gain)
    gate_pre = lowered_backward(project(rescaled_activations, lowered_copy(gate_weight)))
    inner_pre = lowered_backward(project(rescaled_activations, lowered_copy(inner_weight)))
    state_pre = lowered_backward(project(rescaled_activations, lowered_copy(state_weight)))
    step_raw = lowered_backward(project(rescaled_activations, lowered_copy(step_weight)))
    channels = jnp.concatenate([inner_pre, state_pre], axis=-1)
    kernel = jnp.concatenate([conv_weight, state_conv_weight], axis=-1)
    conv_offset = jnp.concatenate([conv_bias, state_conv_bias], axis=-1)
    padded = jnp.pad(channels, ((0, 0), (CONV - 1, 0), (0, 0)))
    conv_out = conv_offset + sum((kernel[tap_index] * padded[:, tap_index:tap_index + length_l] for tap_index in range(CONV)))
    activated = jax.nn.silu(conv_out)
    inner_width = HEADS * HEADDIM
    inputs_x = activated[..., :inner_width].reshape(num_seqs, length_l, HEADS, HEADDIM)
    write_in = activated[..., inner_width:inner_width + STATE]
    read_in = activated[..., inner_width + STATE:]
    step_size = jax.nn.softplus(step_raw + step_bias)
    decay_rate = -jnp.exp(log_rate)
    num_blocks = length_l // GROUP

    def to_blocks(values):
        return jnp.moveaxis(values.reshape((num_seqs, num_blocks, GROUP) + values.shape[2:]), 1, 0)
    step_blocks = jnp.swapaxes(to_blocks(step_size), 2, 3)
    start_state = jnp.zeros((num_seqs, HEADS, STATE, HEADDIM), jnp.float32)
    step_fn = jax.checkpoint(partial(group_step, decay_rate, skip_gain))
    final_state, mixer_blocks = lax.scan(step_fn, start_state, (to_blocks(inputs_x), to_blocks(write_in), to_blocks(read_in), step_blocks))
    mixer = jnp.moveaxis(mixer_blocks, 0, 1).reshape(num_seqs, length_l, inner_width)
    gated = mixer * jax.nn.silu(gate_pre)
    scaling_factor = lax.rsqrt(lax.optimization_barrier(jnp.mean(gated * gated, axis=-1, keepdims=True)) + EPS)
    mixed_output = lowered_copy(gated * scaling_factor * out_gain)
    output_branch = lowered_backward(jnp.einsum('mpo,bo->mpb', mixed_output, lowered_copy(output_projection_weight), precision=FINE_ARITHMETIC))
    return hidden + output_branch

def reference(hidden, norm_gain, gate_weight, inner_weight, state_weight, step_weight, conv_weight, conv_bias, state_conv_weight, state_conv_bias, step_bias, log_rate, skip_gain, out_gain, output_projection_weight, cotangent):
    output, pullback = jax.vjp(forward, hidden, norm_gain, gate_weight, inner_weight, state_weight, step_weight, conv_weight, conv_bias, state_conv_weight, state_conv_bias, step_bias, log_rate, skip_gain, out_gain, output_projection_weight)
    grads = pullback(cotangent)
    return (output, grads[0], grads[1], grads[2], grads[3], grads[4], grads[5], grads[6], grads[7], grads[8], grads[9], grads[10], grads[11], grads[12], grads[13], grads[14])
```

```python
import functools
import math

import jax
import jax.numpy as jnp
from jax import lax
from jax.experimental import pallas as pl
from jax.experimental.pallas import tpu as pltpu
from jax.sharding import Mesh, PartitionSpec as P

EPS = 1e-05
WAYS = 4
LANES = 128
EDGE = 16
TILE = 128
MIB = 1024 * 1024
PLANE, PART, HEAD = "plane", "part", "head"
BLOCK, PLACE, SEQ, ALL = range(4)
F32 = jnp.float32
BF16 = jnp.bfloat16


def cost_of(us):
    return pl.CostEstimate(flops=1024, bytes_accessed=int(us * 3.5e6), transcendentals=0)


def mm(spec, a, b):
    return jnp.einsum(spec, a, b, preferred_element_type=F32)


def flip(value, axis, by):
    size = lax.axis_size(axis)
    return lax.ppermute(value, axis, [(i, i ^ by) for i in range(size)])


def shift(value, axis, by):
    size = lax.axis_size(axis)
    pairs = [(i, i + by) for i in range(size) if 0 <= i + by < size]
    return lax.ppermute(value, axis, pairs)


def total(value, axes, start=1):
    for axis in axes:
        step, start = start, 1
        while step < lax.axis_size(axis):
            value = value + flip(value, axis, step)
            step *= 2
    return value


def take(value, index, axis=0):
    return lax.dynamic_index_in_dim(value, index, axis, False)


def reorder(value, index):
    return jnp.stack([take(value, index[i]) for i in range(value.shape[0])])


def both_cores(value, core):
    other = flip(value, HEAD, 1)
    return jnp.where(core == 0, jnp.stack([value, other]), jnp.stack([other, value]))


def dot(a, b):
    return lax.dot_general(a, b, (((1,), (0,)), ((), ())), preferred_element_type=F32)


def dot_nt(a, b):
    return lax.dot_general(a, b, (((1,), (1,)), ((), ())), preferred_element_type=F32)


def dot_tn(a, b):
    return lax.dot_general(a, b, (((0,), (0,)), ((), ())), preferred_element_type=F32)


def terms_of(value, count):
    parts = []
    for _ in range(count):
        part = value.astype(BF16)
        parts.append(part)
        value = value - part.astype(F32)
    return parts


def fine_dot(product, a, b):
    left = terms_of(a, 2) if a.dtype == F32 else [a]
    right = terms_of(b, 2) if b.dtype == F32 else [b]
    value = product(left[0], right[0])
    for part in left[1:]:
        value = value + product(part, right[0])
    for part in right[1:]:
        value = value + product(left[0], part)
    return value


def triangle_sum(size, reverse, value):
    row = lax.broadcasted_iota(jnp.int32, (size, size), 0)
    col = lax.broadcasted_iota(jnp.int32, (size, size), 1)
    ones = jnp.where(row <= col if reverse else row >= col, 1.0, 0.0).astype(BF16)
    return sum(dot(ones, part) for part in terms_of(value, 3))


def head_lanes(cols, width):
    at = lax.broadcasted_iota(jnp.int32, (LANES, cols), 1) - width * lax.broadcasted_iota(
        jnp.int32, (LANES, cols), 0
    )
    return jnp.where(jnp.logical_and(at >= 0, at < width), 1.0, 0.0).astype(BF16)


def spread_heads(value, table):
    return sum(dot(part, table) for part in terms_of(value, 2))


def sum_heads(value, table):
    return sum(dot_nt(part, table) for part in terms_of(value, 2))


def pack(leaving, run, run_decay):
    cols = run.shape[0]
    leaving[0, :cols] = run[...]
    leaving[0, cols:] = run_decay[...]


def unpack(came, run, width):
    cols = run.shape[0]
    run[...] = jnp.zeros_like(run)
    for ref in reversed(came):
        decay = ref[0, cols : cols + 1]
        for h in range(cols // width):
            at = slice(h * width, (h + 1) * width)
            run[at] = ref[0, at] + decay[:, h : h + 1] * run[at]


def conv_kernel(width, order, pre, halo, taps, offset, step, rate, act, conv, cum, cum_t, step_t, state, leaving, ext, run, run_decay):
    b = pl.program_id(1)
    size, wide = conv.shape[1:]
    tail_rows = ext.shape[0] - size
    count = taps.shape[0]

    @pl.when(b == 0)
    def _():
        ext[:tail_rows] = halo[0]
        run[...] = jnp.zeros_like(run)
        run_decay[...] = jnp.ones_like(run_decay)

    @pl.when(b > 0)
    def _():
        ext[:tail_rows] = ext[size:]

    ext[tail_rows:] = pre[0, :, :wide]
    first = tail_rows - count + 1
    value = offset[...] + sum(taps[k : k + 1] * ext[first + k : first + k + size] for k in range(count))
    conv[0] = value
    active = value * jax.nn.sigmoid(value)
    act[0] = active
    cols = run.shape[0]
    lanes = run.shape[1]
    steps = step[0]
    total_decay = triangle_sum(size, False, steps * rate[...])
    cum[0] = total_decay
    cum_t[0] = total_decay.T[: cum_t.shape[1]]
    step_t[0] = steps.T[: cum_t.shape[1]]
    last = total_decay[size - 1 : size]
    tail = spread_heads(jnp.exp(last - total_decay) * steps, head_lanes(cols, width))
    decay = jnp.exp(last)
    scaled = (active[:, :cols].astype(BF16).astype(F32) * tail).T
    added = fine_dot(dot, scaled, active[:, cols : cols + lanes])
    state[0] = added
    for h in range(cols // width):
        at = slice(h * width, (h + 1) * width)
        run[at] = decay[:, h : h + 1] * run[at] + added[at]
    run_decay[...] = run_decay[...] * decay
    pack(leaving, run, run_decay)


def decay_block(column, row, masked):
    value = column - row
    if masked:
        at = lax.broadcasted_iota(jnp.int32, value.shape, 0)
        value = jnp.where(at >= lax.broadcasted_iota(jnp.int32, value.shape, 1), value, -1e30)
    return jnp.exp(value)


def diagonal_kernel(width, order, act, cum, cum_t, step_t, diagonal, scores, weights):
    size, cols = diagonal.shape[1:]
    lanes = (act.shape[2] - cols) // 2
    heads = cols // width
    low_x = act[0, :, :cols].astype(BF16)
    low_write = act[0, :, cols : cols + lanes].astype(BF16)
    low_read = act[0, :, cols + lanes :].astype(BF16)
    scores[...] = dot_nt(low_read, low_write)

    @pl.when(jnp.logical_and(pl.program_id(0) == 0, pl.program_id(1) == 0))
    def _():
        weights[...] = jnp.zeros_like(weights)

    for h in range(heads):
        for top in range(0, size, TILE):
            rows = slice(top, top + TILE)
            column = cum[0, rows, h : h + 1]
            for left in range(0, top + TILE, TILE):
                span = slice(left, left + TILE)
                table = decay_block(column, cum_t[0, h : h + 1, span], left == top)
                value = scores[rows, span] * table * step_t[0, h : h + 1, span]
                weights[h, rows, span] = value.astype(BF16)
        at = slice(h * width, (h + 1) * width)
        diagonal[0, :, at] = dot(weights[h], low_x[:, at])


def mixer_kernel(width, order, act, cum, diagonal, state, gate, grad, skip, gain, *rest):
    *came, mixer, incoming, sums, run = rest
    size, cols = mixer.shape[1:]
    lanes = run.shape[1]

    @pl.when(pl.program_id(1) == 0)
    def _():
        unpack(came, run, width)

    held = run[...]
    incoming[0] = held
    low_held = held.astype(BF16)
    growth = jnp.exp(cum[0])
    offdiag = fine_dot(dot_nt, act[0, :, cols + lanes :], low_held)
    offdiag = spread_heads(growth, head_lanes(cols, width)) * offdiag
    for h in range(cols // width):
        at = slice(h * width, (h + 1) * width)
        run[at] = growth[size - 1 : size, h : h + 1] * held[at] + state[0, at]
    mixed = diagonal[0] + offdiag + skip[...] * act[0, :, :cols]
    mixer[0] = mixed
    gates = gate[0]
    gated = mixed * (gates * jax.nn.sigmoid(gates))
    square = jnp.sum(gated * gated, axis=1, keepdims=True)
    cross = jnp.sum(grad[0] * gain[...] * gated, axis=1, keepdims=True)
    lane = lax.broadcasted_iota(jnp.int32, (size, LANES), 1)
    both = jnp.where(lane == 0, square, jnp.where(lane == 1, cross, 0.0))
    sums[0] = both.T[: sums.shape[1]]


def gate_kernel(width, inner_total, order, mixer, gate, grad, act, cum, sums, gain, mixed, mixer_grad, gate_low, add, leaving, gain_sum, skip_sum, run, run_decay):
    size, cols = mixed.shape[1:]
    lanes = run.shape[1]
    first = jnp.logical_and(pl.program_id(0) == 0, pl.program_id(1) == 0)

    @pl.when(first)
    def _():
        gain_sum[...] = jnp.zeros_like(gain_sum)
        skip_sum[...] = jnp.zeros_like(skip_sum)

    @pl.when(pl.program_id(1) == 0)
    def _():
        run[...] = jnp.zeros_like(run)
        run_decay[...] = jnp.ones_like(run_decay)

    turned = sums[0].T
    factor = lax.rsqrt(turned[:, 0:1] / inner_total + EPS)
    cross = turned[:, 1:2] / inner_total
    gates = gate[0]
    sigma = jax.nn.sigmoid(gates)
    opened = gates * sigma
    value = mixer[0]
    gated = value * opened
    scaled = gated * factor
    mixed[0] = (scaled * gain[...]).astype(BF16)
    grads = grad[0]
    gain_sum[...] += jnp.sum(grads * scaled, axis=0, keepdims=True)
    gated_grad = factor * (grads * gain[...]) - gated * (factor * factor * factor) * cross
    through = gated_grad * opened
    mixer_grad[0] = through
    gate_low[0] = (gated_grad * value * (sigma * (1.0 + gates * (1.0 - sigma)))).astype(BF16)
    skip_sum[...] += jnp.sum(through * act[0, :, :cols], axis=0, keepdims=True)
    growth = jnp.exp(cum[0])
    low = through.astype(BF16).astype(F32)
    grown = (low * spread_heads(growth, head_lanes(cols, width))).T
    added = fine_dot(dot, grown, act[0, :, cols + lanes :])
    add[0] = added
    for h in range(cols // width):
        at = slice(h * width, (h + 1) * width)
        run[at] = growth[size - 1 : size, h : h + 1] * run[at] + added[at]
    run_decay[...] = run_decay[...] * growth[size - 1 : size]
    pack(leaving, run, run_decay)


def back_kernel(
    width, order, act, conv, pre, cum, cum_t, step, step_t, sigma, mixer_grad, incoming, add, halo, taps, rate, skip, *rest
):
    *came, chan_low, edge, first_rows, taps_sum, bias_sum, rate_sum, step_sum, run, ext, scores, weights, score_sum, by_col = rest
    s, b = pl.program_id(0), pl.program_id(1)
    size, wide = act.shape[1:]
    cols, lanes = run.shape
    tail_rows = ext.shape[0] - size
    count = taps.shape[0]

    @pl.when(jnp.logical_and(s == 0, b == 0))
    def _():
        for ref in (taps_sum, bias_sum, rate_sum, step_sum):
            ref[...] = jnp.zeros_like(ref)

    @pl.when(b == 0)
    def _():
        unpack(came, run, width)
        ext[size:] = jnp.zeros((tail_rows, wide), F32)

    @pl.when(b > 0)
    def _():
        ext[size:] = ext[:tail_rows]

    heads = cols // width
    active = act[0]
    low_x = active[:, :cols].astype(BF16)
    low_write = active[:, cols : cols + lanes].astype(BF16)
    low_read = active[:, cols + lanes :].astype(BF16)
    scores[...] = dot_nt(low_read, low_write)
    outgoing = run[...]
    low_out = outgoing.astype(BF16)
    low_held = incoming[0].astype(BF16)
    grads = mixer_grad[0]
    low_grad = grads.astype(BF16)
    turned = grads.T.astype(BF16)
    decays = cum[0]
    last = decays[size - 1 : size]
    steps = step[0]
    growth = jnp.exp(decays)
    tail_decay = jnp.exp(last - decays)
    tail = tail_decay * steps
    block_decay = jnp.exp(last)

    @pl.when(jnp.logical_and(s == 0, b == 0))
    def _():
        weights[...] = jnp.zeros_like(weights)
        score_sum[...] = jnp.zeros_like(score_sum)
        by_col[...] = jnp.zeros_like(by_col)

    lane = lax.broadcasted_iota(jnp.int32, (TILE, LANES), 1)
    row_tiles = [jnp.zeros((TILE, LANES), F32) for _ in range(size // TILE)]
    pieces = []
    for h in range(heads):
        at = slice(h * width, (h + 1) * width)
        col = slice(h, h + 1)
        grads_w = dot_nt(low_grad[:, at], low_x[:, at])
        col_sums = [jnp.zeros((1, TILE), F32) for _ in range(size // TILE)]
        for i, top in enumerate(range(0, size, TILE)):
            rows = slice(top, top + TILE)
            column = decays[rows, col]
            across = jnp.zeros((TILE, TILE), F32)
            for j, left in enumerate(range(0, top + TILE, TILE)):
                span = slice(left, left + TILE)
                table = decay_block(column, cum_t[0, col, span], left == top)
                step_row = step_t[0, col, span]
                score = scores[rows, span]
                weights[h, rows, span] = (score * table * step_row).astype(BF16)
                eased = grads_w[rows, span] * table
                stepped = eased * step_row
                if h == 0:
                    score_sum[rows, span] = stepped
                else:
                    score_sum[rows, span] += stepped
                col_sums[j] = col_sums[j] + jnp.sum(eased * score, axis=0, keepdims=True)
                across = across + stepped * score
            row_tiles[i] = jnp.where(
                lane == h, jnp.sum(across, axis=1, keepdims=True), row_tiles[i]
            )
        by_col[col] = jnp.concatenate(col_sums, axis=1)
        pieces.append(dot(turned[at], weights[h]))
    by_row = jnp.concatenate(row_tiles, axis=0)

    table = head_lanes(cols, width)
    tail_all = spread_heads(tail, table)
    growth_all = spread_heads(growth, table)
    write_out = fine_dot(dot_nt, active[:, cols : cols + lanes], low_out)
    read_held = fine_dot(dot_nt, active[:, cols + lanes :], low_held)
    tail_grad = sum_heads(low_x.astype(F32) * write_out, table)
    read_dot = sum_heads(low_grad.astype(F32) * read_held, table)
    score_low = score_sum[...].astype(BF16)
    write_sum = fine_dot(dot, low_x.astype(F32) * tail_all, low_out)
    write_sum = write_sum + dot_tn(score_low, low_read)
    read_sum = fine_dot(dot, low_grad.astype(F32) * growth_all, low_held)
    read_sum = read_sum + dot(score_low, low_write)
    pair = jnp.sum(outgoing * incoming[0], axis=1, keepdims=True)
    lane_row = lax.broadcasted_iota(jnp.int32, (1, LANES), 1)
    state_dot = jnp.zeros((1, LANES), F32)
    for h in range(heads):
        at = slice(h * width, (h + 1) * width)
        col = slice(h, h + 1)
        state_dot = jnp.where(lane_row == h, jnp.sum(pair[at], axis=0, keepdims=True), state_dot)
        run[at] = block_decay[:, col] * outgoing[at] + add[0, at]

    pad = jnp.zeros((LANES - by_col.shape[0], size), F32)
    step_grad = jnp.concatenate([by_col[...], pad], axis=0).T
    tail_through = tail_grad * tail
    row_index = lax.broadcasted_iota(jnp.int32, (size, LANES), 0)
    at_last = jnp.sum(tail_through, axis=0, keepdims=True) + state_dot * block_decay
    cum_grad = by_row - steps * step_grad - tail_through + growth * read_dot
    cum_grad = cum_grad + jnp.where(row_index == size - 1, at_last, 0.0)
    rate_grad = triangle_sum(size, True, cum_grad)
    step_grad = step_grad + tail_grad * tail_decay + rate_grad * rate[...]
    rate_sum[...] += jnp.sum(rate_grad * steps, axis=0, keepdims=True) * rate[...]
    raw = step_grad * sigma[0]
    chan_low[0, :, wide:] = raw.astype(BF16)
    step_sum[...] += jnp.sum(raw, axis=0, keepdims=True)

    x_grad = jnp.concatenate(pieces, axis=0).T + write_out * tail_all + skip[...] * grads
    value = conv[0]
    sig = jax.nn.sigmoid(value)
    slope = sig * (1.0 + value * (1.0 - sig))
    conv_grad = jnp.concatenate([x_grad, write_sum, read_sum], axis=1) * slope
    ext[:size] = conv_grad
    bias_sum[...] += jnp.sum(conv_grad, axis=0, keepdims=True)
    channels = pre[0]
    channel_grad = jnp.zeros((size, wide), F32)
    for k in range(count):
        moved = ext[count - 1 - k : count - 1 - k + size]
        channel_grad = channel_grad + taps[k : k + 1] * moved
        taps_sum[k : k + 1] += jnp.sum(channels * moved, axis=0, keepdims=True)
    chan_low[0, :, :wide] = channel_grad.astype(BF16)

    @pl.when(b == 0)
    def _():
        edge[0] = channel_grad[size - EDGE :]

    @pl.when(b == pl.num_programs(1) - 1)
    def _():
        first_rows[0] = conv_grad[:8]
        for k in range(count - 1):
            have = count - 1 - k
            taps_sum[k : k + 1] += jnp.sum(
                halo[0, 8 - have :] * conv_grad[:have], axis=0, keepdims=True
            )


def gather_kernel(ranges, core, own, *refs):
    others = 2 * (WAYS - 1)
    near, far = refs[: WAYS - 1], refs[WAYS - 1 : others]
    table, tokens, *results = refs[others:]
    step = tokens.shape[0]
    sources = [None, *near, None, *far]
    for at in range(0, 2 * WAYS, step):

        @pl.when(pl.program_id(0) == at // step)
        def _(at=at):
            for j in range(step):
                ref = sources[at + j]
                if ref is None:
                    tokens[j] = own[lax.rem(core[0] + (at + j) // WAYS, 2)]
                else:
                    tokens[j] = ref[...]

    rows = flat_rows(tokens)
    for (at, size), result in zip(ranges, results):
        result[...] = dot(rows, table[:, at : at + size]).reshape(result.shape)


def rows_kernel(columns, tokens, table, result):
    at, size = columns
    result[...] = dot(flat_rows(tokens), table[:, at : at + size]).reshape(result.shape)


def join_kernel(ranges, summed, *refs):
    count = len(ranges)
    lows, arrived, tables, others = [refs[j * count : (j + 1) * count] for j in range(4)]
    value = None
    for low, table, at_size in zip((*lows, *arrived), (*tables, *others), ranges + ranges):
        at, size = at_size
        term = dot_nt(flat_rows(low), table[:, at : at + size])
        value = term if value is None else value + term
    if summed:
        tokens, keep_a, keep_b, send_a, send_b, gain_sum = refs[4 * count :]

        @pl.when(pl.program_id(0) == 0)
        def _():
            gain_sum[...] = jnp.zeros_like(gain_sum)

        gain_sum[...] += jnp.sum(value * flat_rows(tokens).astype(F32), axis=0, keepdims=True)
    else:
        keep_a, keep_b, send_a, send_b = refs[4 * count :]
    size, half = keep_a.shape[1:]

    @pl.when(pl.program_id(0) == 0)
    def _():
        keep_a[0] = value[:size, :half]
        keep_b[0] = value[:size, half:]
        send_a[0] = value[size:, :half].astype(BF16)
        keep_b[1] = value[size:, half:]

    @pl.when(pl.program_id(0) == 1)
    def _():
        keep_a[1] = value[:size, :half]
        send_b[0] = value[:size, half:].astype(BF16)
        send_a[1] = value[size:, :half].astype(BF16)
        send_b[1] = value[size:, half:].astype(BF16)


def middle_kernel(keep_a, keep_b, got_a, got_b, send_a, send_b):
    send_a[...] = (keep_a[0] + got_a[0].astype(F32)).astype(BF16)
    send_b[...] = (keep_b[0] + got_b[0].astype(F32)).astype(BF16)


def flat_rows(ref):
    value = ref[...]
    return value.reshape(value.shape[0] * value.shape[1], value.shape[2])


def store_tiles(result, at, value):
    count, _, deep = result.shape
    for i in range(count):
        result[i, at : at + value.shape[0]] = value[:, i * deep : (i + 1) * deep].astype(
            result.dtype
        )


def early_grad_kernel(tokens, gate_low, cot_low, mixed, result, turned):
    cols = gate_low.shape[2]

    @pl.when(pl.program_id(0) == 0)
    def _():
        turned[:cols] = flat_rows(gate_low).T
        turned[cols:] = flat_rows(mixed).T

    store_tiles(result, 0, dot(turned[:cols], flat_rows(tokens)))
    store_tiles(result, cols, dot(turned[cols:], flat_rows(cot_low)))


def late_grad_kernel(core, tokens, chan_low, inner, mine, other, step, turned):
    cols, lanes = inner.shape[1], mine.shape[1]
    wide = cols + 2 * lanes

    @pl.when(pl.program_id(0) == 0)
    def _():
        turned[...] = flat_rows(chan_low).T

    rows = flat_rows(tokens)
    store_tiles(inner, 0, dot(turned[:cols], rows))
    write = dot(turned[cols : cols + lanes], rows)
    read = dot(turned[cols + lanes : wide], rows)
    swap = core[0] != 0
    store_tiles(mine, 0, jnp.where(swap, read, write))
    store_tiles(other, 0, jnp.where(swap, write, read))
    store_tiles(step, 0, dot(turned[wide : wide + step.shape[1]], rows))


def chunk_kernel(plane, inner, mine, arrived, step, own, *sent):
    k = pl.program_id(0)
    cols, lanes = inner.shape[1], mine.shape[1]
    state = mine[0] + arrived[0]

    @pl.when(k == 0)
    def _():
        own[:cols] = inner[0].astype(F32)
        own[cols : cols + lanes] = state
        own[cols + lanes :] = step[0].astype(F32)

    for j, ref in enumerate(sent):

        @pl.when(k == j + 1)
        def _(ref=ref):
            ref[:cols] = inner[0]
            ref[cols : cols + lanes] = state.astype(BF16)
            ref[cols + lanes :] = step[0]


def turn_kernel(cols, lanes, part, early, own, *refs):
    count = (len(refs) - 1 - WAYS) if len(refs) > WAYS else 0
    value = own[...]
    for ref in refs[:count]:
        value = value + ref[...].astype(F32)
    pieces, turned = refs[count:-1], refs[-1]
    value = value.T
    wide = early.shape[0]
    turned[:, :wide] = early[...].astype(F32).T
    turned[:, wide : wide + cols] = value[:, :cols]
    state = value[:, cols : cols + lanes]
    high = state.astype(BF16).astype(F32)
    at = wide + cols
    turned[:, at : at + lanes] = high
    turned[:, at + lanes : at + 2 * lanes] = state - high
    turned[:, at + 2 * lanes :] = value[:, cols + lanes :]
    for k, ref in enumerate(pieces):
        size = ref.shape[0]
        first = pl.multiple_of((part[0] ^ k) * size, 8)
        ref[...] = turned[pl.ds(first, size)].astype(BF16)


def place_kernel(part, *refs):
    pieces = [ref[...].astype(F32) for ref in refs[:WAYS]]
    gate, out, inner, state, step = refs[WAYS:]
    lanes = state.shape[1]
    at = 0
    for result in (gate, out, inner):
        size = result.shape[1] // WAYS
        for k, piece in enumerate(pieces):
            to = pl.multiple_of((part[0] ^ k) * size, LANES)
            result[:, pl.ds(to, size)] = piece[:, at : at + size]
        at += size
    state[...] = sum(piece[:, at : at + lanes] + piece[:, at + lanes : at + 2 * lanes] for piece in pieces)
    at += 2 * lanes
    size = step.shape[1] // WAYS
    for j in range(WAYS):
        value = pieces[0][:, at : at + size]
        for k in range(1, WAYS):
            value = jnp.where((part[0] ^ k) == j, pieces[k][:, at : at + size], value)
        step[:, j * size : (j + 1) * size] = value


def pair_kernel(core, mine, other, base, result):
    same = pl.program_id(0) == core[0]

    @pl.when(same)
    def _():
        result[0] = base[0] + mine[...]

    @pl.when(jnp.logical_not(same))
    def _():
        result[0] = base[0] + other[...]


def pinned(value, near):
    space = pltpu.VMEM if near else pltpu.HBM
    return pltpu.with_memory_space_constraint(value, space)


def result(shape, dtype, near):
    return (pltpu.VMEM if near else pltpu.HBM)(shape, dtype)


def plain_call(body, grid, ins, outs, load, scalars=(), scratch=(), near=(), near_outs=()):
    us, mib = load
    ins = [(pinned(v, i in near), *r) for i, (v, *r) in enumerate(ins)]

    def spec(shape, block, index, once=True):
        if block is None:
            mode = {"pipeline_mode": pl.Buffered(1)} if once and len(shape) > 1 else {}
            return pl.BlockSpec(shape, lambda *a: (0,) * len(shape), **mode)
        return pl.BlockSpec(block, lambda *a: index(*a[: len(grid)]))

    return pl.pallas_call(
        body,
        grid_spec=pltpu.PrefetchScalarGridSpec(
            num_scalar_prefetch=len(scalars),
            grid=grid,
            in_specs=[spec(v.shape, block, index) for v, block, index in ins],
            out_specs=[spec(shape, block, index, False) for shape, _, block, index in outs],
            scratch_shapes=[pltpu.VMEM(shape, dtype) for shape, dtype in scratch],
        ),
        out_shape=[
            result(shape, dtype, i in near_outs) for i, (shape, dtype, _, _) in enumerate(outs)
        ],
        compiler_params=pltpu.CompilerParams(
            dimension_semantics=("arbitrary",) * len(grid), vmem_limit_bytes=mib * MIB
        ),
        cost_estimate=cost_of(us),
    )(*scalars, *[v for v, _, _ in ins])


def whole(value):
    return (value, None, None)


def rows_of(value):
    return (value, (1,) + value.shape[1:], lambda i: (i, 0, 0))


def plane_send(core, own):
    mine = take(own, core[0])
    return [flip(mine, PART, k) for k in range(1, WAYS)]


def gathered_matmul(core, own, near, table, ranges, load, near_outs):
    _, size, depth = own.shape
    far = [flip(value, HEAD, 1) for value in near]
    blocks, step = 2 * WAYS, 2

    def out(cols, dtype):
        return ((blocks, size, cols), dtype, (step, size, cols), lambda i: (i, 0, 0))

    return plain_call(
        functools.partial(gather_kernel, ranges),
        (blocks // step,),
        [whole(v) for v in [own] + near + far + [table]],
        [out(depth, BF16)] + [out(cols, F32) for _, cols in ranges],
        load,
        scalars=(core,),
        near_outs=near_outs,
    )


def token_matmul(tokens, table, columns, load):
    blocks, size, depth = tokens.shape
    cols, step = columns[1], 2
    return plain_call(
        functools.partial(rows_kernel, columns),
        (blocks // step,),
        [(tokens, (step, size, depth), lambda i: (i, 0, 0)), whole(table)],
        [((blocks, size, cols), F32, (step, size, cols), lambda i: (i, 0, 0))],
        load,
        near_outs=(0,),
    )[0]


def to_other_core(lows):
    return [flip(low[WAYS:], HEAD, 1) for low in lows]


def join_matmul(lows, arrived, tables, others, ranges, tokens, load, near, near_outs):
    _, size, _ = lows[0].shape
    depth = tables[0].shape[0]

    def block(v):
        return (v, (2,) + v.shape[1:], lambda i: (i, 0, 0))

    half = (2, size, depth // 2)
    ins = [block(v) for v in lows + arrived] + [whole(t) for t in tables + others]
    outs = [(half, dtype, None, None) for dtype in (F32, F32, BF16, BF16)]
    if tokens is not None:
        ins.append(block(tokens))
        outs.append(((1, depth), F32, None, None))
    return plain_call(
        functools.partial(join_kernel, ranges, tokens is not None),
        (WAYS // 2,),
        ins,
        outs,
        load,
        near=near,
        near_outs=near_outs,
    )


def plane_middle(merged, done, load):
    keep_a, keep_b, send_a, send_b = merged
    keep_a, keep_b = after((keep_a, keep_b), done)
    _, size, half = keep_a.shape
    got_a = flip(send_a, PART, 1)
    got_b = flip(send_b, PART, 2)
    block = (1, size, half)
    sent = plain_call(
        middle_kernel,
        (1,),
        [(v, block, lambda i: (1, 0, 0)) for v in (keep_a, keep_b, got_a, got_b)],
        [((size, half), BF16, None, None)] * 2,
        load,
    )
    return (keep_a, keep_b, got_a, got_b), sent


def plane_sum(parts, sent):
    keep_a, keep_b, got_a, got_b = parts
    a = keep_a[0] + got_a[0].astype(F32) + flip(sent[0], PART, 2).astype(F32)
    b = keep_b[0] + got_b[0].astype(F32) + flip(sent[1], PART, 1).astype(F32)
    return jnp.concatenate([a, b], axis=1)


def pair_add(core, mine, base, load):
    other = flip(mine, HEAD, 1)
    seqs, size, depth = base.shape
    tile = size // 2
    flat = ((tile, depth), lambda i, j: (j, 0))
    deep = ((1, tile, depth), lambda i, j: (i, j, 0))
    return plain_call(
        pair_kernel,
        (seqs, size // tile),
        [(mine, *flat), (other, *flat), (base, *deep)],
        [(base.shape, F32, *deep)],
        load,
        scalars=(core,),
        near=(0, 1),
    )[0]


def after(value, done):
    return lax.optimization_barrier((value, done))[0]


def place_spec(kind, shape, reverse):
    def place(s, b):
        return s * WAYS + (WAYS - 1 - b if reverse else b)

    if kind == ALL:
        return pl.BlockSpec(shape, lambda s, b, o: (0,) * len(shape))
    block = (1,) + tuple(shape[1:])
    if kind == SEQ:
        return pl.BlockSpec(block, lambda s, b, o: (s, 0, 0))
    if kind == PLACE:
        return pl.BlockSpec(block, lambda s, b, o: (place(s, b), 0, 0))
    return pl.BlockSpec(block, lambda s, b, o: (o[place(s, b)], 0, 0))


def block_call(body, order, num_seqs, ins, outs, scratch, reverse, load, near=(), near_outs=()):
    us, mib = load

    ins = [(kind, pinned(v, i in near)) for i, (kind, v) in enumerate(ins)]
    return pl.pallas_call(
        body,
        grid_spec=pltpu.PrefetchScalarGridSpec(
            num_scalar_prefetch=1,
            grid=(num_seqs, WAYS),
            in_specs=[place_spec(kind, v.shape, reverse) for kind, v in ins],
            out_specs=[place_spec(kind, shape, reverse) for kind, shape, _ in outs],
            scratch_shapes=[pltpu.VMEM(shape, dtype) for shape, dtype in scratch],
        ),
        out_shape=[result(shape, dtype, i in near_outs) for i, (_, shape, dtype) in enumerate(outs)],
        compiler_params=pltpu.CompilerParams(
            dimension_semantics=("arbitrary", "arbitrary"), vmem_limit_bytes=mib * MIB
        ),
        cost_estimate=cost_of(us),
    )(order, *[v for _, v in ins])


def per_device(
    hidden,
    norm_gain,
    gate_weight,
    inner_weight,
    state_weight,
    step_weight,
    conv_weight,
    conv_bias,
    state_conv_weight,
    state_conv_bias,
    step_bias,
    log_rate,
    skip_gain,
    out_gain,
    output_projection_weight,
    cotangent,
):
    num_seqs, block_len, model_width = hidden.shape
    planes = lax.axis_size(PLANE)
    rows = gate_weight.shape[0]
    cols = gate_weight.shape[1] // WAYS
    heads = step_bias.shape[0] // WAYS
    width = cols // heads
    state = state_weight.shape[1] // 2
    taps = conv_weight.shape[0]
    inner_total = cols * WAYS * lax.axis_size(HEAD)
    length = WAYS * block_len
    plane = lax.axis_index(PLANE)
    part = lax.axis_index(PART)
    core = lax.axis_index(HEAD)
    core_at = core.astype(jnp.int32)[None]
    blocks = num_seqs * WAYS
    order = jnp.stack(
        [(s ^ core) * WAYS + (b ^ part) for s in range(num_seqs) for b in range(WAYS)]
    ).astype(jnp.int32)
    ring = jnp.arange(WAYS) ^ part

    def my_cols(value, axis, which=None):
        size = value.shape[axis] // WAYS
        at = part if which is None else which
        return lax.dynamic_slice_in_dim(value, at * size, size, axis)

    def pad_heads(value):
        return jnp.pad(value, (0, LANES - heads))[None]

    def to_owner(tables):
        def piece(which):
            return jnp.concatenate([t(which) for t in tables], axis=1)

        got = [piece(part)] + [flip(piece(part ^ k), PART, k) for k in range(1, WAYS)]
        return got[-1], reorder(jnp.stack(got), ring).reshape(WAYS * rows, -1)

    def cut(value):
        return lambda which: my_cols(value, 1, which)

    mixed_cols = cols + 2 * state
    low_state = state_weight.astype(BF16)
    low_step = step_weight.astype(BF16)
    first = mixed_cols + LANES
    arrived, first_rows = to_owner(
        [
            cut(inner_weight.astype(BF16)),
            lambda which: low_state,
            lambda which: jnp.pad(my_cols(low_step, 1, which), ((0, 0), (0, LANES - heads))),
        ]
    )
    inv_rms = lax.rsqrt(jnp.mean(hidden * hidden, axis=-1, keepdims=True) + EPS)
    unit_rows = hidden * inv_rms
    normed = (unit_rows * norm_gain).astype(BF16)
    near = plane_send(core_at, normed)
    in_rows = lax.all_gather(first_rows, PLANE, axis=0, tiled=True)
    later = after((gate_weight, output_projection_weight), near)
    arrived, late_rows = to_owner([cut(later[0].astype(BF16)), cut(later[1].astype(BF16))])
    late_rows = lax.all_gather(late_rows, PLANE, axis=0, tiled=True)
    cot_own = after(cotangent, arrived).astype(BF16)
    cot_near = plane_send(core_at, cot_own)
    tokens, pre, step_raw = gathered_matmul(
        core_at, normed, near, in_rows, [(0, mixed_cols), (mixed_cols, LANES)], (10, 20), ()
    )

    ends = [
        lax.dynamic_slice(
            pre, (order[s * WAYS + WAYS - 1], block_len - 8, 0), (1, 8, mixed_cols)
        )
        for s in range(num_seqs)
    ]
    halo = shift(jnp.concatenate(ends), PLANE, 1)
    taps_all = jnp.concatenate([my_cols(conv_weight, 1), state_conv_weight], axis=1)
    offset = jnp.concatenate([my_cols(conv_bias, 0), state_conv_bias])[None]
    pre_step = step_raw + pad_heads(my_cols(step_bias, 0))
    step_size = jax.nn.softplus(pre_step)
    step_slope = jax.nn.sigmoid(pre_step)
    rate = pad_heads(-jnp.exp(my_cols(log_rate, 0)))
    skip = jnp.repeat(my_cols(skip_gain, 0), width)[None]
    gain = my_cols(out_gain, 0)[None]

    call = functools.partial(block_call, order=order, num_seqs=num_seqs)
    tall = (blocks, block_len, LANES)
    square = (block_len, block_len)
    flat = (blocks, 8, block_len)
    inner = (blocks, block_len, cols)
    states = (blocks, cols, state)
    message = (num_seqs, cols + 8, state)
    act, conv, cum, cum_t, step_t, group_state, leaving = call(
        functools.partial(conv_kernel, width),
        ins=[
            (BLOCK, pre),
            (SEQ, halo),
            (ALL, taps_all),
            (ALL, offset),
            (BLOCK, step_size),
            (ALL, rate),
        ],
        outs=[
            (BLOCK, (blocks, block_len, mixed_cols), F32),
            (BLOCK, (blocks, block_len, mixed_cols), F32),
            (BLOCK, tall, F32),
            (BLOCK, flat, F32),
            (BLOCK, flat, F32),
            (PLACE, states, F32),
            (SEQ, message, F32),
        ],
        scratch=[((block_len + 8, mixed_cols), F32), ((cols, state), F32), ((8, LANES), F32)],
        reverse=False,
        load=(11, 14),
        near_outs=(0, 2),
    )
    came = [shift(leaving, PLANE, 1)]
    (diagonal,) = call(
        functools.partial(diagonal_kernel, width),
        ins=[(BLOCK, act), (BLOCK, cum), (BLOCK, cum_t), (BLOCK, step_t)],
        outs=[(BLOCK, inner, F32)],
        scratch=[(square, F32), ((heads,) + square, BF16)],
        reverse=False,
        load=(5, 14),
        near=(0, 1),
    )
    came.append(shift(after(came[0], diagonal), PLANE, 1))
    gate_pre = token_matmul(after(tokens, came[0]), late_rows, (0, cols), (5, 14))
    came.append(shift(after(came[1], gate_pre), PLANE, 1))
    cot_low, mixed_grad = gathered_matmul(
        core_at, after(cot_own, came[1]), after(cot_near, diagonal), late_rows, [(cols, cols)], (7, 20), (1,)
    )
    for _ in range(4, planes):
        came.append(shift(came[-1], PLANE, 1))
    mixer, incoming, sums = call(
        functools.partial(mixer_kernel, width),
        ins=[
            (BLOCK, act),
            (BLOCK, cum),
            (BLOCK, diagonal),
            (PLACE, group_state),
            (BLOCK, gate_pre),
            (BLOCK, mixed_grad),
            (ALL, skip),
            (ALL, gain),
        ]
        + [(SEQ, v) for v in came],
        outs=[(BLOCK, inner, F32), (PLACE, states, F32), (PLACE, flat, F32)],
        scratch=[((cols, state), F32)],
        reverse=False,
        load=(9, 14),
        near=(0, 1, 4, 5),
        near_outs=(0,),
    )
    sums = total(sums, (HEAD, PART))
    late_other = flip(after(late_rows, sums), HEAD, 1)
    in_other = flip(after(in_rows, late_other), HEAD, 1)
    mixed, mixer_grad, gate_low, state_add, leaving, gain_sum, skip_sum = call(
        functools.partial(gate_kernel, width, inner_total),
        ins=[
            (BLOCK, mixer),
            (BLOCK, gate_pre),
            (BLOCK, mixed_grad),
            (BLOCK, act),
            (BLOCK, cum),
            (PLACE, sums),
            (ALL, gain),
        ],
        outs=[
            (BLOCK, inner, BF16),
            (BLOCK, inner, F32),
            (BLOCK, inner, BF16),
            (PLACE, states, F32),
            (SEQ, message, F32),
            (ALL, (1, cols), F32),
            (ALL, (1, cols), F32),
        ],
        scratch=[((cols, state), F32), ((8, LANES), F32)],
        reverse=True,
        load=(10, 14),
        near=(0, 1, 2, 3, 4),
    )
    came = [shift(leaving, PLANE, -1)]
    mixed_got = to_other_core([mixed])
    deep = WAYS * rows

    group = LANES // math.gcd(deep, LANES)

    def tile(value):
        return (value, (blocks, block_len, group * deep), lambda i: (0, 0, i))

    (early_w,) = plain_call(
        early_grad_kernel,
        (planes // group,),
        [tile(tokens), whole(gate_low), tile(cot_low), whole(mixed)],
        [((planes, 2 * cols, deep), BF16, (group, 2 * cols, deep), lambda i: (i, 0, 0))],
        (9, 24),
        scratch=[((2 * cols, blocks * block_len), BF16)],
    )
    came.append(shift(after(came[0], early_w), PLANE, -1))
    out_merged = join_matmul(
        [mixed], after(mixed_got, came[0]), [late_rows], [late_other], [(cols, cols)], None, (6, 24), (3,), ()
    )
    came.append(shift(after(came[1], out_merged), PLANE, -1))
    for _ in range(4, planes):
        came.append(shift(came[-1], PLANE, -1))
    early_rows = lax.psum_scatter(
        after(early_w, came), PLANE, scatter_dimension=0, tiled=True
    )
    gate_got = to_other_core([gate_low])
    mixer_grad = after(mixer_grad, (out_merged[2:], in_other))
    chan_low, edge, first_rows, taps_sum, bias_sum, rate_sum, step_sum = call(
        functools.partial(back_kernel, width),
        ins=[
            (BLOCK, act),
            (BLOCK, conv),
            (BLOCK, pre),
            (BLOCK, cum),
            (BLOCK, cum_t),
            (BLOCK, step_size),
            (BLOCK, step_t),
            (BLOCK, step_slope),
            (BLOCK, mixer_grad),
            (PLACE, incoming),
            (PLACE, state_add),
            (SEQ, halo),
            (ALL, taps_all),
            (ALL, rate),
            (ALL, skip),
        ]
        + [(SEQ, v) for v in came],
        outs=[
            (BLOCK, (blocks, block_len, first), BF16),
            (SEQ, (num_seqs, EDGE, mixed_cols), F32),
            (SEQ, (num_seqs, 8, mixed_cols), F32),
            (ALL, (8, mixed_cols), F32),
            (ALL, (1, mixed_cols), F32),
            (ALL, (1, LANES), F32),
            (ALL, (1, LANES), F32),
        ],
        scratch=[
            ((cols, state), F32),
            ((block_len + 8, mixed_cols), F32),
            (square, F32),
            ((heads,) + square, BF16),
            (square, F32),
            ((8, block_len), F32),
        ],
        reverse=True,
        load=(28, 22),
        near_outs=(0,),
    )
    following = shift(first_rows, PLANE, -1)
    late = jnp.concatenate([jnp.zeros_like(edge), following], axis=1)
    fix = sum(taps_all[k] * late[:, taps - 1 - k : taps - 1 - k + EDGE] for k in range(taps))
    fixed = after((edge + fix).astype(BF16), early_rows)
    for s in range(num_seqs):
        chan_low = lax.dynamic_update_slice(
            chan_low, fixed[s : s + 1], (order[s * WAYS + WAYS - 1], block_len - EDGE, 0)
        )
    out_parts, out_sent = plane_middle(out_merged, chan_low, (2, 14))
    part_at = part.astype(jnp.int32)[None]

    def exchanged(pieces):
        return [pieces[0]] + [flip(pieces[k], PART, k) for k in range(1, WAYS)]

    chan_low, out_sent, gate_got = lax.optimization_barrier((chan_low, out_sent, gate_got))
    low_got = gate_got + to_other_core([chan_low])
    out_mine = plane_sum(out_parts, out_sent)

    inner_w, state_w, state_other, step_w = plain_call(
        late_grad_kernel,
        (planes // group,),
        [tile(tokens), whole(chan_low)],
        [
            ((planes, c, deep), dtype, (group, c, deep), lambda i: (i, 0, 0))
            for c, dtype in ((cols, BF16), (state, F32), (state, F32), (EDGE, BF16))
        ],
        (9, 22),
        near=(1,),
        scalars=(core_at,),
        scratch=[((first, blocks * block_len), BF16)],
    )
    arrived = flip(state_other, HEAD, 1)
    plane_at = plane.astype(jnp.int32)[None]
    tall = cols + state + EDGE

    def crossed(value):
        block = (1,) + value.shape[1:]
        return pl.BlockSpec(block, lambda k, p: (p[0] ^ k, 0, 0))

    def flat_out(dtype):
        return jax.ShapeDtypeStruct((tall, deep), dtype)

    own_chunk, *sent_chunks = pl.pallas_call(
        chunk_kernel,
        grid_spec=pltpu.PrefetchScalarGridSpec(
            num_scalar_prefetch=1,
            grid=(planes,),
            in_specs=[crossed(v) for v in (inner_w, state_w, arrived, step_w)],
            out_specs=[pl.BlockSpec((tall, deep), lambda k, p: (0, 0))] * planes,
        ),
        out_shape=[flat_out(F32)] + [flat_out(BF16)] * (planes - 1),
        compiler_params=pltpu.CompilerParams(
            dimension_semantics=("arbitrary",), vmem_limit_bytes=8 * MIB
        ),
        cost_estimate=cost_of(3),
    )(plane_at, inner_w, state_w, arrived, step_w)
    got_chunks = [flip(v, PLANE, k + 1) for k, v in enumerate(sent_chunks)]
    *normed_merged, gain_local = join_matmul(
        [after(gate_low, own_chunk), chan_low],
        low_got,
        [late_rows, in_rows],
        [late_other, in_other],
        [(0, cols), (0, first)],
        tokens,
        (11, 30),
        (1, 2, 3, 6, 7),
        (0, 1, 2, 3),
    )
    output = pair_add(core_at, out_mine, hidden, (4, 14))
    keep_a, keep_b, send_a, send_b = normed_merged
    send_a, send_b = after((send_a, send_b), got_chunks[0::2])
    normed_merged = (keep_a, keep_b, send_a, send_b)
    shared = jnp.concatenate(
        [taps_sum[:taps, cols:].reshape(-1), bias_sum[0, cols:], gain_local[0]]
    )
    own = jnp.concatenate(
        [
            taps_sum[:taps, :cols].reshape(-1),
            bias_sum[0, :cols],
            gain_sum[0],
            step_sum[0, :heads],
            rate_sum[0, :heads],
            jnp.sum(skip_sum.reshape(heads, width), axis=1),
        ]
    )
    slots = jnp.where(jnp.arange(WAYS)[:, None] == part, own[None], 0.0)
    shared = total(shared, (HEAD,))
    vector = jnp.concatenate([shared, slots.reshape(-1)])
    normed_parts, normed_sent = plane_middle(
        normed_merged, (got_chunks[1::2], output), (2, 14)
    )
    late_pieces = plain_call(
        functools.partial(turn_kernel, cols, state),
        (1,),
        [whole(v) for v in [early_rows[0], own_chunk] + got_chunks],
        [((rows, 2 * cols + tall + state), BF16, None, None)] * WAYS,
        (3, 16),
        scalars=(part_at,),
        scratch=[((deep, 2 * cols + tall + state), F32)],
    )
    normed_parts = after(normed_parts, late_pieces)
    late_got = exchanged(late_pieces)
    normed_grad = plane_sum(normed_parts, normed_sent)
    unit_mine = take(unit_rows, core)
    unit_grad = normed_grad * norm_gain
    hidden_mine = take(inv_rms, core) * (
        unit_grad - unit_mine * jnp.mean(unit_grad * unit_mine, axis=-1, keepdims=True)
    )
    hidden_grad = pair_add(core_at, hidden_mine, cotangent, (4, 14))
    gate_weight_grad, out_weight_grad, inner_weight_grad, state_mine, step_weight_grad = plain_call(
        place_kernel,
        (1,),
        [whole(v) for v in late_got],
        [
            ((rows, size), F32, None, None)
            for size in (WAYS * cols, WAYS * cols, WAYS * cols, state, WAYS * heads)
        ],
        (4, 16),
        scalars=(part_at,),
    )
    state_weight_grad = jnp.moveaxis(both_cores(state_mine, core), 0, 1).reshape(rows, -1)
    vector = total(after(vector, normed_parts), (PLANE,))
    vector = total(after(vector, hidden_grad), (PART,))
    shared = vector[: shared.shape[0]]
    slots = vector[shared.shape[0] :].reshape(WAYS, -1)
    at = [taps * cols, (taps + 1) * cols, (taps + 2) * cols]
    conv_weight_grad = jnp.moveaxis(slots[:, : at[0]].reshape(WAYS, taps, cols), 0, 1).reshape(
        taps, -1
    )
    conv_bias_grad = slots[:, at[0] : at[1]].reshape(-1)
    out_gain_grad = slots[:, at[1] : at[2]].reshape(-1)
    step_bias_grad = slots[:, at[2] : at[2] + heads].reshape(-1)
    log_rate_grad = slots[:, at[2] + heads : at[2] + 2 * heads].reshape(-1)
    skip_gain_grad = slots[:, at[2] + 2 * heads : at[2] + 3 * heads].reshape(-1)
    state_conv = shared[: (taps + 1) * 2 * state].reshape(taps + 1, 2 * state)
    norm_gain_grad = shared[(taps + 1) * 2 * state :] / norm_gain

    return (
        output,
        hidden_grad,
        norm_gain_grad,
        gate_weight_grad,
        inner_weight_grad,
        state_weight_grad,
        step_weight_grad,
        conv_weight_grad,
        conv_bias_grad,
        state_conv[:taps],
        state_conv[taps],
        step_bias_grad,
        log_rate_grad,
        skip_gain_grad,
        out_gain_grad,
        out_weight_grad,
    )


def solution(mesh):
    grid = mesh.devices
    fine = Mesh(
        grid.reshape(grid.shape[0] // WAYS, WAYS, grid.shape[1]), (PLANE, PART, HEAD)
    )
    seq = (PLANE, PART)
    tokens, table, columns = P(None, seq, None), P(seq, HEAD), P(HEAD)
    return jax.shard_map(
        per_device,
        mesh=fine,
        in_specs=(
            tokens,
            P(),
            table,
            table,
            P(seq, None),
            table,
            P(None, HEAD),
            columns,
            P(),
            P(),
            columns,
            columns,
            columns,
            columns,
            table,
            tokens,
        ),
        out_specs=(
            tokens,
            tokens,
            P(),
            table,
            table,
            P(seq, None),
            table,
            P(None, HEAD),
            columns,
            P(),
            P(),
            columns,
            columns,
            columns,
            columns,
            table,
        ),
        check_vma=False,
    )
```

```python
import functools
import math

import jax
import jax.numpy as jnp
from jax import lax
from jax.experimental import pallas as pl
from jax.experimental.pallas import tpu as pltpu
from jax.sharding import Mesh, PartitionSpec as P

EPS = 1e-05
WAYS = 4
LANES = 128
EDGE = 16
MIB = 1024 * 1024
PLANE, PART, HEAD = "plane", "part", "head"
BLOCK, PLACE, SEQ, ALL = range(4)
F32 = jnp.float32
BF16 = jnp.bfloat16


def cost_of(us):
    return pl.CostEstimate(flops=1024, bytes_accessed=int(us * 3.5e6), transcendentals=0)


def mm(spec, a, b):
    return jnp.einsum(spec, a, b, preferred_element_type=F32)


def flip(value, axis, by):
    size = lax.axis_size(axis)
    return lax.ppermute(value, axis, [(i, i ^ by) for i in range(size)])


def shift(value, axis, by):
    size = lax.axis_size(axis)
    pairs = [(i, i + by) for i in range(size) if 0 <= i + by < size]
    return lax.ppermute(value, axis, pairs)


def total(value, axes, start=1):
    for axis in axes:
        step, start = start, 1
        while step < lax.axis_size(axis):
            value = value + flip(value, axis, step)
            step *= 2
    return value


def take(value, index, axis=0):
    return lax.dynamic_index_in_dim(value, index, axis, False)


def reorder(value, index):
    return jnp.stack([take(value, index[i]) for i in range(value.shape[0])])


def dot(a, b):
    return lax.dot_general(a, b, (((1,), (0,)), ((), ())), preferred_element_type=F32)


def dot_nt(a, b):
    return lax.dot_general(a, b, (((1,), (1,)), ((), ())), preferred_element_type=F32)


def dot_tn(a, b):
    return lax.dot_general(a, b, (((0,), (0,)), ((), ())), preferred_element_type=F32)


def terms_of(value, count):
    parts = []
    for _ in range(count):
        part = value.astype(BF16)
        parts.append(part)
        value = value - part.astype(F32)
    return parts


def fine_dot(product, a, b):
    left = terms_of(a, 2) if a.dtype == F32 else [a]
    right = terms_of(b, 2) if b.dtype == F32 else [b]
    value = product(left[0], right[0])
    for part in left[1:]:
        value = value + product(part, right[0])
    for part in right[1:]:
        value = value + product(left[0], part)
    return value


def triangle_sum(size, reverse, value):
    row = lax.broadcasted_iota(jnp.int32, (size, size), 0)
    col = lax.broadcasted_iota(jnp.int32, (size, size), 1)
    ones = jnp.where(row <= col if reverse else row >= col, 1.0, 0.0).astype(BF16)
    return sum(dot(ones, part) for part in terms_of(value, 3))


def head_lanes(cols, width):
    at = lax.broadcasted_iota(jnp.int32, (LANES, cols), 1) - width * lax.broadcasted_iota(
        jnp.int32, (LANES, cols), 0
    )
    return jnp.where(jnp.logical_and(at >= 0, at < width), 1.0, 0.0).astype(BF16)


def spread_heads(value, table):
    return sum(dot(part, table) for part in terms_of(value, 2))


def sum_heads(value, table):
    return sum(dot_nt(part, table) for part in terms_of(value, 2))


def to_columns(rows):
    pad = jnp.zeros((LANES - rows.shape[0], rows.shape[1]), F32)
    return jnp.concatenate([rows, pad], axis=0).T


def pack(leaving, run, run_decay):
    cols = run.shape[0]
    leaving[0, :cols] = run[...]
    leaving[0, cols:] = run_decay[...]


def unpack(came, run, width):
    cols = run.shape[0]
    run[...] = jnp.zeros_like(run)
    for ref in reversed(came):
        decay = ref[0, cols : cols + 1]
        for h in range(cols // width):
            at = slice(h * width, (h + 1) * width)
            run[at] = ref[0, at] + decay[:, h : h + 1] * run[at]


def conv_kernel(width, order, pre, halo, taps, offset, step, rate, act, conv, cum, cum_t, state, leaving, ext, run, run_decay):
    b = pl.program_id(1)
    size, wide = conv.shape[1:]
    tail_rows = ext.shape[0] - size
    count = taps.shape[0]

    @pl.when(b == 0)
    def _():
        ext[:tail_rows] = halo[0]
        run[...] = jnp.zeros_like(run)
        run_decay[...] = jnp.ones_like(run_decay)

    @pl.when(b > 0)
    def _():
        ext[:tail_rows] = ext[size:]

    ext[tail_rows:] = pre[0, :, :wide]
    first = tail_rows - count + 1
    value = offset[...] + sum(taps[k : k + 1] * ext[first + k : first + k + size] for k in range(count))
    conv[0] = value
    active = value * jax.nn.sigmoid(value)
    act[0] = active
    cols = run.shape[0]
    lanes = run.shape[1]
    steps = to_columns(step[0])
    total_decay = triangle_sum(size, False, steps * rate[...])
    cum[0] = total_decay
    cum_t[0] = total_decay.T[: cum_t.shape[1]]
    last = total_decay[size - 1 : size]
    tail = spread_heads(jnp.exp(last - total_decay) * steps, head_lanes(cols, width))
    decay = jnp.exp(last)
    scaled = (active[:, :cols].astype(BF16).astype(F32) * tail).T
    added = fine_dot(dot, scaled, active[:, cols : cols + lanes])
    state[0] = added
    for h in range(cols // width):
        at = slice(h * width, (h + 1) * width)
        run[at] = decay[:, h : h + 1] * run[at] + added[at]
    run_decay[...] = run_decay[...] * decay
    pack(leaving, run, run_decay)


def lower(size):
    row = lax.broadcasted_iota(jnp.int32, (size, size), 0)
    return row >= lax.broadcasted_iota(jnp.int32, (size, size), 1)


def diagonal_kernel(width, order, act, cum, cum_t, step_t, diagonal):
    size, cols = diagonal.shape[1:]
    lanes = (act.shape[2] - cols) // 2
    low_x = act[0, :, :cols].astype(BF16)
    low_write = act[0, :, cols : cols + lanes].astype(BF16)
    low_read = act[0, :, cols + lanes :].astype(BF16)
    scores = dot_nt(low_read, low_write)
    mask = lower(size)
    for h in range(cols // width):
        at = slice(h * width, (h + 1) * width)
        table = jnp.exp(jnp.where(mask, cum[0, :, h : h + 1] - cum_t[0, h : h + 1], -1e30))
        weights = (scores * table * step_t[0, h : h + 1]).astype(BF16)
        diagonal[0, :, at] = dot(weights, low_x[:, at])


def mixer_kernel(width, order, act, cum, diagonal, state, gate, grad, skip, gain, *rest):
    *came, mixer, incoming, sums, run = rest
    size, cols = mixer.shape[1:]
    lanes = run.shape[1]

    @pl.when(pl.program_id(1) == 0)
    def _():
        unpack(came, run, width)

    held = run[...]
    incoming[0] = held
    low_held = held.astype(BF16)
    growth = jnp.exp(cum[0])
    offdiag = fine_dot(dot_nt, act[0, :, cols + lanes :], low_held)
    offdiag = spread_heads(growth, head_lanes(cols, width)) * offdiag
    for h in range(cols // width):
        at = slice(h * width, (h + 1) * width)
        run[at] = growth[size - 1 : size, h : h + 1] * held[at] + state[0, at]
    mixed = diagonal[0] + offdiag + skip[...] * act[0, :, :cols]
    mixer[0] = mixed
    gates = gate[0]
    gated = mixed * (gates * jax.nn.sigmoid(gates))
    square = jnp.sum(gated * gated, axis=1, keepdims=True)
    cross = jnp.sum(grad[0] * gain[...] * gated, axis=1, keepdims=True)
    lane = lax.broadcasted_iota(jnp.int32, (size, LANES), 1)
    both = jnp.where(lane == 0, square, jnp.where(lane == 1, cross, 0.0))
    sums[0] = both.T[: sums.shape[1]]


def gate_kernel(width, inner_total, order, mixer, gate, grad, act, cum, sums, gain, mixed, mixer_grad, gate_low, add, leaving, gain_sum, run, run_decay):
    size, cols = mixed.shape[1:]
    lanes = run.shape[1]
    first = jnp.logical_and(pl.program_id(0) == 0, pl.program_id(1) == 0)

    @pl.when(first)
    def _():
        gain_sum[...] = jnp.zeros_like(gain_sum)

    @pl.when(pl.program_id(1) == 0)
    def _():
        run[...] = jnp.zeros_like(run)
        run_decay[...] = jnp.ones_like(run_decay)

    turned = sums[0].T
    factor = lax.rsqrt(turned[:, 0:1] / inner_total + EPS)
    cross = turned[:, 1:2] / inner_total
    gates = gate[0]
    sigma = jax.nn.sigmoid(gates)
    opened = gates * sigma
    value = mixer[0]
    gated = value * opened
    scaled = gated * factor
    mixed[0] = (scaled * gain[...]).astype(BF16)
    grads = grad[0]
    gain_sum[0:1] += jnp.sum(grads * scaled, axis=0, keepdims=True)
    gated_grad = factor * (grads * gain[...]) - gated * (factor * factor * factor) * cross
    through = gated_grad * opened
    mixer_grad[0] = through
    gate_low[0] = (gated_grad * value * (sigma * (1.0 + gates * (1.0 - sigma)))).astype(BF16)
    gain_sum[1:2] += jnp.sum(through * act[0, :, :cols], axis=0, keepdims=True)
    growth = jnp.exp(cum[0])
    low = through.astype(BF16).astype(F32)
    grown = (low * spread_heads(growth, head_lanes(cols, width))).T
    added = fine_dot(dot, grown, act[0, :, cols + lanes :])
    add[0] = added
    for h in range(cols // width):
        at = slice(h * width, (h + 1) * width)
        run[at] = growth[size - 1 : size, h : h + 1] * run[at] + added[at]
    run_decay[...] = run_decay[...] * growth[size - 1 : size]
    pack(leaving, run, run_decay)


def back_kernel(
    width, order, act, conv, pre, cum, cum_t, step_t, sigma, mixer_grad, incoming, add, halo, taps, rate, skip, *rest
):
    *came, chan_low, edge, first_rows, taps_sum, run, ext = rest
    s, b = pl.program_id(0), pl.program_id(1)
    size, wide = act.shape[1:]
    cols, lanes = run.shape
    tail_rows = ext.shape[0] - size
    count = taps.shape[0]

    @pl.when(jnp.logical_and(s == 0, b == 0))
    def _():
        taps_sum[...] = jnp.zeros_like(taps_sum)

    @pl.when(b == 0)
    def _():
        unpack(came, run, width)
        ext[size:] = jnp.zeros((tail_rows, wide), F32)

    @pl.when(b > 0)
    def _():
        ext[size:] = ext[:tail_rows]

    heads = cols // width
    active = act[0]
    low_x = active[:, :cols].astype(BF16)
    low_write = active[:, cols : cols + lanes].astype(BF16)
    low_read = active[:, cols + lanes :].astype(BF16)
    scores = dot_nt(low_read, low_write)
    mask = lower(size)
    outgoing = run[...]
    low_out = outgoing.astype(BF16)
    low_held = incoming[0].astype(BF16)
    grads = mixer_grad[0]
    low_grad = grads.astype(BF16)
    turned = grads.T.astype(BF16)
    decays = cum[0]
    last = decays[size - 1 : size]
    steps = to_columns(step_t[0])
    growth = jnp.exp(decays)
    tail_decay = jnp.exp(last - decays)
    tail = tail_decay * steps
    block_decay = jnp.exp(last)

    lane = lax.broadcasted_iota(jnp.int32, (size, LANES), 1)
    row8 = lax.broadcasted_iota(jnp.int32, cum_t.shape[1:], 0)
    by_row = jnp.zeros((size, LANES), F32)
    by_col = jnp.zeros(cum_t.shape[1:], F32)
    score_sum = jnp.zeros((size, size), F32)
    pieces = []
    for h in range(heads):
        at = slice(h * width, (h + 1) * width)
        col = slice(h, h + 1)
        table = jnp.exp(jnp.where(mask, decays[:, col] - cum_t[0, col], -1e30))
        step_row = step_t[0, col]
        weights = (scores * table * step_row).astype(BF16)
        eased = dot_nt(low_grad[:, at], low_x[:, at]) * table
        stepped = eased * step_row
        score_sum = score_sum + stepped
        by_col = jnp.where(row8 == h, jnp.sum(eased * scores, axis=0, keepdims=True), by_col)
        by_row = jnp.where(lane == h, jnp.sum(stepped * scores, axis=1, keepdims=True), by_row)
        pieces.append(dot(turned[at], weights))

    table = head_lanes(cols, width)
    tail_all = spread_heads(tail, table)
    growth_all = spread_heads(growth, table)
    write_out = fine_dot(dot_nt, active[:, cols : cols + lanes], low_out)
    read_held = fine_dot(dot_nt, active[:, cols + lanes :], low_held)
    tail_grad = sum_heads(low_x.astype(F32) * write_out, table)
    read_dot = sum_heads(low_grad.astype(F32) * read_held, table)
    score_low = score_sum.astype(BF16)
    write_sum = fine_dot(dot, low_x.astype(F32) * tail_all, low_out)
    write_sum = write_sum + dot_tn(score_low, low_read)
    read_sum = fine_dot(dot, low_grad.astype(F32) * growth_all, low_held)
    read_sum = read_sum + dot(score_low, low_write)
    pair = jnp.sum(outgoing * incoming[0], axis=1, keepdims=True)
    lane_row = lax.broadcasted_iota(jnp.int32, (1, LANES), 1)
    state_dot = jnp.zeros((1, LANES), F32)
    for h in range(heads):
        at = slice(h * width, (h + 1) * width)
        col = slice(h, h + 1)
        state_dot = jnp.where(lane_row == h, jnp.sum(pair[at], axis=0, keepdims=True), state_dot)
        run[at] = block_decay[:, col] * outgoing[at] + add[0, at]

    pad = jnp.zeros((LANES - by_col.shape[0], size), F32)
    step_grad = jnp.concatenate([by_col, pad], axis=0).T
    tail_through = tail_grad * tail
    row_index = lax.broadcasted_iota(jnp.int32, (size, LANES), 0)
    at_last = jnp.sum(tail_through, axis=0, keepdims=True) + state_dot * block_decay
    cum_grad = by_row - steps * step_grad - tail_through + growth * read_dot
    cum_grad = cum_grad + jnp.where(row_index == size - 1, at_last, 0.0)
    rate_grad = triangle_sum(size, True, cum_grad)
    step_grad = step_grad + tail_grad * tail_decay + rate_grad * rate[...]
    taps_sum[count + 1 : count + 2, LANES : 2 * LANES] += (
        jnp.sum(rate_grad * steps, axis=0, keepdims=True) * rate[...]
    )
    raw = step_grad * to_columns(sigma[0])
    chan_low[0, :, wide:] = raw.astype(BF16)
    taps_sum[count + 1 : count + 2, :LANES] += jnp.sum(raw, axis=0, keepdims=True)

    x_grad = jnp.concatenate(pieces, axis=0).T + write_out * tail_all + skip[...] * grads
    value = conv[0]
    sig = jax.nn.sigmoid(value)
    slope = sig * (1.0 + value * (1.0 - sig))
    conv_grad = jnp.concatenate([x_grad, write_sum, read_sum], axis=1) * slope
    ext[:size] = conv_grad
    taps_sum[count : count + 1] += jnp.sum(conv_grad, axis=0, keepdims=True)
    channels = pre[0]
    channel_grad = jnp.zeros((size, wide), F32)
    for k in range(count):
        moved = ext[count - 1 - k : count - 1 - k + size]
        channel_grad = channel_grad + taps[k : k + 1] * moved
        taps_sum[k : k + 1] += jnp.sum(channels * moved, axis=0, keepdims=True)
    chan_low[0, :, :wide] = channel_grad.astype(BF16)

    @pl.when(b == 0)
    def _():
        edge[0] = channel_grad[size - EDGE :]

    @pl.when(b == pl.num_programs(1) - 1)
    def _():
        first_rows[0] = conv_grad[:8]
        for k in range(count - 1):
            have = count - 1 - k
            taps_sum[k : k + 1] += jnp.sum(
                halo[0, 8 - have :] * conv_grad[:have], axis=0, keepdims=True
            )


def gather_kernel(ranges, core, own, *refs):
    others = 2 * (WAYS - 1)
    near, far = refs[: WAYS - 1], refs[WAYS - 1 : others]
    table, tokens, *results = refs[others:]
    step = tokens.shape[0]
    sources = [None, *near, None, *far]
    for at in range(0, 2 * WAYS, step):

        @pl.when(pl.program_id(0) == at // step)
        def _(at=at):
            for j in range(step):
                ref = sources[at + j]
                if ref is None:
                    tokens[j] = own[lax.rem(core[0] + (at + j) // WAYS, 2)]
                else:
                    tokens[j] = ref[...]

    rows = flat_rows(tokens)
    for (at, size), result in zip(ranges, results):
        value = dot(rows, table[:, at : at + size])
        if result.shape[2] == size:
            result[...] = value.reshape(result.shape)
        else:
            for j in range(step):
                turned = value[j * result.shape[2] : (j + 1) * result.shape[2]].T
                result[j] = turned[: result.shape[1]]


def rows_kernel(columns, tokens, table, result):
    at, size = columns
    result[...] = dot(flat_rows(tokens), table[:, at : at + size]).reshape(result.shape)


def join_kernel(ranges, summed, *refs):
    count = len(ranges)
    lows, arrived, tables, others = [refs[j * count : (j + 1) * count] for j in range(4)]
    value = None
    for low, table, at_size in zip((*lows, *arrived), (*tables, *others), ranges + ranges):
        at, size = at_size
        term = dot_nt(flat_rows(low), table[:, at : at + size])
        value = term if value is None else value + term
    if summed:
        tokens, keep_a, keep_b, send_a, send_b, gain_sum = refs[4 * count :]

        @pl.when(pl.program_id(0) == 0)
        def _():
            gain_sum[...] = jnp.zeros_like(gain_sum)

        sums = jnp.sum(value * flat_rows(tokens).astype(F32), axis=0, keepdims=True)
        span = gain_sum.shape[1]
        for r in range(WAYS):
            gain_sum[r : r + 1] += sums[:, r * span : (r + 1) * span]
    else:
        keep_a, keep_b, send_a, send_b = refs[4 * count :]
    size, half = keep_a.shape[1:]

    @pl.when(pl.program_id(0) == 0)
    def _():
        keep_a[0] = value[:size, :half]
        keep_b[0] = value[:size, half:]
        send_a[0] = value[size:, :half].astype(BF16)
        keep_b[1] = value[size:, half:]

    @pl.when(pl.program_id(0) == 1)
    def _():
        keep_a[1] = value[:size, :half]
        send_b[0] = value[:size, half:].astype(BF16)
        send_a[1] = value[size:, :half].astype(BF16)
        send_b[1] = value[size:, half:].astype(BF16)


def middle_kernel(keep_a, keep_b, got_a, got_b, send_a, send_b):
    send_a[...] = (keep_a[0] + got_a[0].astype(F32)).astype(BF16)
    send_b[...] = (keep_b[0] + got_b[0].astype(F32)).astype(BF16)


def flat_rows(ref):
    value = ref[...]
    return value.reshape(value.shape[0] * value.shape[1], value.shape[2])


def store_tiles(result, at, value):
    count, _, deep = result.shape
    for i in range(count):
        result[i, at : at + value.shape[0]] = value[:, i * deep : (i + 1) * deep].astype(
            result.dtype
        )


def early_grad_kernel(tokens, gate_low, cot_low, mixed, result, turned):
    cols = gate_low.shape[2]

    @pl.when(pl.program_id(0) == 0)
    def _():
        turned[:cols] = flat_rows(gate_low).T
        turned[cols:] = flat_rows(mixed).T

    store_tiles(result, 0, dot(turned[:cols], flat_rows(tokens)))
    store_tiles(result, cols, dot(turned[cols:], flat_rows(cot_low)))


def late_grad_kernel(core, tokens, chan_low, inner, mine, other, step, turned):
    cols, lanes = inner.shape[1], mine.shape[1]
    wide = cols + 2 * lanes

    @pl.when(pl.program_id(0) == 0)
    def _():
        turned[...] = flat_rows(chan_low).T

    rows = flat_rows(tokens)
    store_tiles(inner, 0, dot(turned[:cols], rows))
    write = dot(turned[cols : cols + lanes], rows)
    read = dot(turned[cols + lanes : wide], rows)
    swap = core[0] != 0
    store_tiles(mine, 0, jnp.where(swap, read, write))
    store_tiles(other, 0, jnp.where(swap, write, read))
    store_tiles(step, 0, dot(turned[wide : wide + step.shape[1]], rows))


def chunk_kernel(plane, inner, mine, arrived, step, own, *sent):
    k = pl.program_id(0)
    cols, lanes = inner.shape[1], mine.shape[1]
    state = mine[0] + arrived[0]

    @pl.when(k == 0)
    def _():
        own[:cols] = inner[0].astype(F32)
        own[cols : cols + lanes] = state
        own[cols + lanes :] = step[0].astype(F32)

    for j, ref in enumerate(sent):

        @pl.when(k == j + 1)
        def _(ref=ref):
            ref[:cols] = inner[0]
            ref[cols : cols + lanes] = state.astype(BF16)
            ref[cols + lanes :] = step[0]


def turn_kernel(cols, lanes, part, small, early, own, *refs):
    count = len(refs) - 1 - WAYS
    value = own[...]
    for ref in refs[:count]:
        value = value + ref[...].astype(F32)
    pieces, turned = refs[count:-1], refs[-1]
    value = value.T
    wide = early.shape[0]
    turned[:, :wide] = early[...].astype(F32).T
    turned[:, wide : wide + cols] = value[:, :cols]
    state = value[:, cols : cols + lanes]
    high = state.astype(BF16).astype(F32)
    at = wide + cols
    turned[:, at : at + lanes] = high
    turned[:, at + lanes : at + 2 * lanes] = state - high
    turned[:, at + 2 * lanes :] = value[:, cols + lanes :]
    size = turned.shape[0] // WAYS
    lines, span = small.shape
    pad = pieces[0].shape[0] - size
    sums = small[...]
    high = sums.astype(BF16).astype(F32)
    rest = jnp.zeros((lines, turned.shape[1] - 2 * span), F32)
    sums = jnp.concatenate([high, sums - high, rest], axis=1)
    below = jnp.zeros((pad - lines, turned.shape[1]), F32)
    sums = jnp.concatenate([sums, below], axis=0).astype(BF16)
    for k, ref in enumerate(pieces):
        first = pl.multiple_of((part[0] ^ k) * size, 8)
        ref[:pad] = sums
        ref[pad:] = turned[pl.ds(first, size)].astype(BF16)


def place_kernel(span, part, *refs):
    gate, out, inner, final, step, convs, bias, gains, heads = refs[WAYS:]
    rows, lanes = gate.shape[0], final.shape[1]
    cols = gate.shape[1] // WAYS
    values = [ref[...].astype(F32) for ref in refs[:WAYS]]
    pad = values[0].shape[0] - rows
    pieces = [value[pad:] for value in values]
    sums = [value[:24, :span] + value[:24, span : 2 * span] for value in values]
    at = 0
    for result in (gate, out, inner):
        for k, piece in enumerate(pieces):
            to = pl.multiple_of((part[0] ^ k) * cols, LANES)
            result[:, pl.ds(to, cols)] = piece[:, at : at + cols]
        at += cols
    final[:rows] = sum(
        piece[:, at : at + lanes] + piece[:, at + lanes : at + 2 * lanes] for piece in pieces
    )
    at += 2 * lanes
    size = step.shape[1] // WAYS
    for j in range(WAYS):
        value = pieces[0][:, at : at + size]
        for k in range(1, WAYS):
            value = jnp.where((part[0] ^ k) == j, pieces[k][:, at : at + size], value)
        step[:, j * size : (j + 1) * size] = value
    shared = sum(sums)
    lines = [shared[i : i + 1, cols + j * lanes : cols + (j + 1) * lanes] for i in range(5) for j in range(2)]
    lines += [
        shared[16 + r : 17 + r, j * lanes : (j + 1) * lanes]
        for r in range(WAYS)
        for j in range(cols // lanes)
    ]
    for i, line in enumerate(lines):
        final[rows + i : rows + i + 1] = line
    left = final.shape[0] - rows - len(lines)
    final[rows + len(lines) :] = jnp.zeros((left, lanes), F32)
    for k, value in enumerate(sums):
        to = pl.multiple_of((part[0] ^ k) * cols, LANES)
        count = convs.shape[0]
        convs[:, pl.ds(to, cols)] = value[:count, :cols]
        bias[:, pl.ds(to, cols)] = value[count : count + 1, :cols]
        gains[:, pl.ds(to, cols)] = value[8:9, :cols]
        skips = sum_heads(value[8:16, :cols], head_lanes(cols, cols // size))
        slot = pl.ds(part[0] ^ k, 1)
        heads[slot] = jnp.concatenate([value[count + 1 : count + 2, : 2 * LANES], skips[1:2]], axis=1)


def pair_kernel(core, mine, other, base, result):
    same = pl.program_id(0) == core[0]

    @pl.when(same)
    def _():
        result[0] = base[0] + mine[...]

    @pl.when(jnp.logical_not(same))
    def _():
        result[0] = base[0] + other[...]


def pinned(value, near):
    space = pltpu.VMEM if near else pltpu.HBM
    return pltpu.with_memory_space_constraint(value, space)


def result(shape, dtype, near):
    return (pltpu.VMEM if near else pltpu.HBM)(shape, dtype)


def plain_call(body, grid, ins, outs, load, scalars=(), scratch=(), near=(), near_outs=()):
    us, mib = load
    ins = [(pinned(v, i in near), *r) for i, (v, *r) in enumerate(ins)]

    def spec(shape, block, index, once=True):
        if block is None:
            mode = {"pipeline_mode": pl.Buffered(1)} if once and len(shape) > 1 else {}
            return pl.BlockSpec(shape, lambda *a: (0,) * len(shape), **mode)
        return pl.BlockSpec(block, lambda *a: index(*a[: len(grid)]))

    return pl.pallas_call(
        body,
        grid_spec=pltpu.PrefetchScalarGridSpec(
            num_scalar_prefetch=len(scalars),
            grid=grid,
            in_specs=[spec(v.shape, block, index) for v, block, index in ins],
            out_specs=[spec(shape, block, index, False) for shape, _, block, index in outs],
            scratch_shapes=[pltpu.VMEM(shape, dtype) for shape, dtype in scratch],
        ),
        out_shape=[
            result(shape, dtype, i in near_outs) for i, (shape, dtype, _, _) in enumerate(outs)
        ],
        compiler_params=pltpu.CompilerParams(
            dimension_semantics=("arbitrary",) * len(grid), vmem_limit_bytes=mib * MIB
        ),
        cost_estimate=cost_of(us),
    )(*scalars, *[v for v, _, _ in ins])


def whole(value):
    return (value, None, None)


def rows_of(value):
    return (value, (1,) + value.shape[1:], lambda i: (i, 0, 0))


def plane_send(core, own):
    mine = take(own, core[0])
    return [flip(mine, PART, k) for k in range(1, WAYS)]


def gathered_matmul(core, own, near, table, ranges, load, near_outs):
    _, size, depth = own.shape
    far = [flip(value, HEAD, 1) for value in near]
    blocks, step = 2 * WAYS, 2

    def out(cols, dtype):
        return ((blocks, size, cols), dtype, (step, size, cols), lambda i: (i, 0, 0))

    rows_out = ((blocks, 8, size), F32, (step, 8, size), lambda i: (i, 0, 0))
    return plain_call(
        functools.partial(gather_kernel, ranges),
        (blocks // step,),
        [whole(v) for v in [own] + near + far + [table]],
        [out(depth, BF16)]
        + [out(cols, F32) if cols > LANES else rows_out for _, cols in ranges],
        load,
        scalars=(core,),
        near_outs=near_outs,
    )


def token_matmul(tokens, table, columns, load):
    blocks, size, depth = tokens.shape
    cols, step = columns[1], 2
    return plain_call(
        functools.partial(rows_kernel, columns),
        (blocks // step,),
        [(tokens, (step, size, depth), lambda i: (i, 0, 0)), whole(table)],
        [((blocks, size, cols), F32, (step, size, cols), lambda i: (i, 0, 0))],
        load,
        near_outs=(0,),
    )[0]


def to_other_core(lows):
    return [flip(low[WAYS:], HEAD, 1) for low in lows]


def join_matmul(lows, arrived, tables, others, ranges, tokens, load, near, near_outs):
    _, size, _ = lows[0].shape
    depth = tables[0].shape[0]

    def block(v):
        return (v, (2,) + v.shape[1:], lambda i: (i, 0, 0))

    half = (2, size, depth // 2)
    ins = [block(v) for v in lows + arrived] + [whole(t) for t in tables + others]
    outs = [(half, dtype, None, None) for dtype in (F32, F32, BF16, BF16)]
    if tokens is not None:
        ins.append(block(tokens))
        outs.append(((8, depth // WAYS), F32, None, None))
    return plain_call(
        functools.partial(join_kernel, ranges, tokens is not None),
        (WAYS // 2,),
        ins,
        outs,
        load,
        near=near,
        near_outs=near_outs,
    )


def plane_middle(merged, done, load):
    keep_a, keep_b, send_a, send_b = merged
    keep_a, keep_b = after((keep_a, keep_b), done)
    _, size, half = keep_a.shape
    got_a = flip(send_a, PART, 1)
    got_b = flip(send_b, PART, 2)
    block = (1, size, half)
    sent = plain_call(
        middle_kernel,
        (1,),
        [(v, block, lambda i: (1, 0, 0)) for v in (keep_a, keep_b, got_a, got_b)],
        [((size, half), BF16, None, None)] * 2,
        load,
    )
    return (keep_a, keep_b, got_a, got_b), sent


def plane_sum(parts, sent):
    keep_a, keep_b, got_a, got_b = parts
    a = keep_a[0] + got_a[0].astype(F32) + flip(sent[0], PART, 2).astype(F32)
    b = keep_b[0] + got_b[0].astype(F32) + flip(sent[1], PART, 1).astype(F32)
    return jnp.concatenate([a, b], axis=1)


def pair_add(core, mine, base, load):
    other = flip(mine, HEAD, 1)
    seqs, size, depth = base.shape
    tile = size // 2
    flat = ((tile, depth), lambda i, j: (j, 0))
    deep = ((1, tile, depth), lambda i, j: (i, j, 0))
    return plain_call(
        pair_kernel,
        (seqs, size // tile),
        [(mine, *flat), (other, *flat), (base, *deep)],
        [(base.shape, F32, *deep)],
        load,
        scalars=(core,),
        near=(0, 1),
    )[0]


def after(value, done):
    return lax.optimization_barrier((value, done))[0]


def place_spec(kind, shape, reverse):
    def place(s, b):
        return s * WAYS + (WAYS - 1 - b if reverse else b)

    if kind == ALL:
        return pl.BlockSpec(shape, lambda s, b, o: (0,) * len(shape))
    block = (1,) + tuple(shape[1:])
    if kind == SEQ:
        return pl.BlockSpec(block, lambda s, b, o: (s, 0, 0))
    if kind == PLACE:
        return pl.BlockSpec(block, lambda s, b, o: (place(s, b), 0, 0))
    return pl.BlockSpec(block, lambda s, b, o: (o[place(s, b)], 0, 0))


def block_call(body, order, num_seqs, ins, outs, scratch, reverse, load, near=(), near_outs=()):
    us, mib = load

    ins = [(kind, pinned(v, i in near)) for i, (kind, v) in enumerate(ins)]
    return pl.pallas_call(
        body,
        grid_spec=pltpu.PrefetchScalarGridSpec(
            num_scalar_prefetch=1,
            grid=(num_seqs, WAYS),
            in_specs=[place_spec(kind, v.shape, reverse) for kind, v in ins],
            out_specs=[place_spec(kind, shape, reverse) for kind, shape, _ in outs],
            scratch_shapes=[pltpu.VMEM(shape, dtype) for shape, dtype in scratch],
        ),
        out_shape=[result(shape, dtype, i in near_outs) for i, (_, shape, dtype) in enumerate(outs)],
        compiler_params=pltpu.CompilerParams(
            dimension_semantics=("arbitrary", "arbitrary"), vmem_limit_bytes=mib * MIB
        ),
        cost_estimate=cost_of(us),
    )(order, *[v for _, v in ins])


def per_device(
    hidden,
    norm_gain,
    gate_weight,
    inner_weight,
    state_weight,
    step_weight,
    conv_weight,
    conv_bias,
    state_conv_weight,
    state_conv_bias,
    step_bias,
    log_rate,
    skip_gain,
    out_gain,
    output_projection_weight,
    cotangent,
):
    num_seqs, block_len, model_width = hidden.shape
    planes = lax.axis_size(PLANE)
    rows = gate_weight.shape[0]
    cols = gate_weight.shape[1] // WAYS
    heads = step_bias.shape[0] // WAYS
    width = cols // heads
    state = state_weight.shape[1] // 2
    taps = conv_weight.shape[0]
    inner_total = cols * WAYS * lax.axis_size(HEAD)
    length = WAYS * block_len
    plane = lax.axis_index(PLANE)
    part = lax.axis_index(PART)
    core = lax.axis_index(HEAD)
    core_at = core.astype(jnp.int32)[None]
    blocks = num_seqs * WAYS
    order = jnp.stack(
        [(s ^ core) * WAYS + (b ^ part) for s in range(num_seqs) for b in range(WAYS)]
    ).astype(jnp.int32)
    ring = jnp.arange(WAYS) ^ part

    def my_cols(value, axis, which=None):
        size = value.shape[axis] // WAYS
        at = part if which is None else which
        return lax.dynamic_slice_in_dim(value, at * size, size, axis)

    def pad_heads(value):
        return jnp.pad(value, (0, LANES - heads))[None]

    def to_owner(tables):
        def piece(which):
            return jnp.concatenate([t(which) for t in tables], axis=1)

        got = [piece(part)] + [flip(piece(part ^ k), PART, k) for k in range(1, WAYS)]
        return got[-1], reorder(jnp.stack(got), ring).reshape(WAYS * rows, -1)

    def cut(value):
        return lambda which: my_cols(value, 1, which)

    mixed_cols = cols + 2 * state
    low_state = state_weight.astype(BF16)
    low_step = step_weight.astype(BF16)
    first = mixed_cols + LANES
    arrived, first_rows = to_owner(
        [
            cut(inner_weight.astype(BF16)),
            lambda which: low_state,
            lambda which: jnp.pad(my_cols(low_step, 1, which), ((0, 0), (0, LANES - heads))),
        ]
    )
    inv_rms = lax.rsqrt(jnp.mean(hidden * hidden, axis=-1, keepdims=True) + EPS)
    unit_rows = hidden * inv_rms
    normed = (unit_rows * norm_gain).astype(BF16)
    near = plane_send(core_at, normed)
    in_rows = lax.all_gather(first_rows, PLANE, axis=0, tiled=True)
    later = after((gate_weight, output_projection_weight), near)
    arrived, late_rows = to_owner([cut(later[0].astype(BF16)), cut(later[1].astype(BF16))])
    late_rows = lax.all_gather(late_rows, PLANE, axis=0, tiled=True)
    cot_own = after(cotangent, arrived).astype(BF16)
    cot_near = plane_send(core_at, cot_own)
    tokens, pre, step_raw = gathered_matmul(
        core_at, normed, near, in_rows, [(0, mixed_cols), (mixed_cols, LANES)], (10, 20), ()
    )

    ends = [
        lax.dynamic_slice(
            pre, (order[s * WAYS + WAYS - 1], block_len - 8, 0), (1, 8, mixed_cols)
        )
        for s in range(num_seqs)
    ]
    halo = shift(jnp.concatenate(ends), PLANE, 1)
    taps_all = jnp.concatenate([my_cols(conv_weight, 1), state_conv_weight], axis=1)
    offset = jnp.concatenate([my_cols(conv_bias, 0), state_conv_bias])[None]
    pre_step = step_raw + jnp.pad(my_cols(step_bias, 0), (0, 8 - heads))[:, None]
    step_size = jax.nn.softplus(pre_step)
    step_slope = jax.nn.sigmoid(pre_step)
    rate = pad_heads(-jnp.exp(my_cols(log_rate, 0)))
    skip = jnp.repeat(my_cols(skip_gain, 0), width)[None]
    gain = my_cols(out_gain, 0)[None]

    call = functools.partial(block_call, order=order, num_seqs=num_seqs)
    tall = (blocks, block_len, LANES)
    flat = (blocks, 8, block_len)
    inner = (blocks, block_len, cols)
    states = (blocks, cols, state)
    message = (num_seqs, cols + 8, state)
    act, conv, cum, cum_t, group_state, leaving = call(
        functools.partial(conv_kernel, width),
        ins=[
            (BLOCK, pre),
            (SEQ, halo),
            (ALL, taps_all),
            (ALL, offset),
            (BLOCK, step_size),
            (ALL, rate),
        ],
        outs=[
            (BLOCK, (blocks, block_len, mixed_cols), F32),
            (BLOCK, (blocks, block_len, mixed_cols), F32),
            (BLOCK, tall, F32),
            (BLOCK, flat, F32),
            (PLACE, states, F32),
            (SEQ, message, F32),
        ],
        scratch=[((block_len + 8, mixed_cols), F32), ((cols, state), F32), ((8, LANES), F32)],
        reverse=False,
        load=(11, 14),
        near_outs=(0, 2),
    )
    came = [shift(leaving, PLANE, 1)]
    (diagonal,) = call(
        functools.partial(diagonal_kernel, width),
        ins=[(BLOCK, act), (BLOCK, cum), (BLOCK, cum_t), (BLOCK, step_size)],
        outs=[(BLOCK, inner, F32)],
        scratch=[],
        reverse=False,
        load=(5, 14),
        near=(0, 1),
    )
    came.append(shift(after(came[0], diagonal), PLANE, 1))
    gate_pre = token_matmul(after(tokens, came[0]), late_rows, (0, cols), (5, 14))
    came.append(shift(after(came[1], gate_pre), PLANE, 1))
    cot_low, mixed_grad = gathered_matmul(
        core_at, after(cot_own, came[1]), after(cot_near, diagonal), late_rows, [(cols, cols)], (7, 20), (1,)
    )
    for _ in range(4, planes):
        came.append(shift(came[-1], PLANE, 1))
    mixer, incoming, sums = call(
        functools.partial(mixer_kernel, width),
        ins=[
            (BLOCK, act),
            (BLOCK, cum),
            (BLOCK, diagonal),
            (PLACE, group_state),
            (BLOCK, gate_pre),
            (BLOCK, mixed_grad),
            (ALL, skip),
            (ALL, gain),
        ]
        + [(SEQ, v) for v in came],
        outs=[(BLOCK, inner, F32), (PLACE, states, F32), (PLACE, flat, F32)],
        scratch=[((cols, state), F32)],
        reverse=False,
        load=(9, 14),
        near=(0, 1, 4, 5),
        near_outs=(0,),
    )
    sums = total(sums, (HEAD, PART))
    late_other = flip(after(late_rows, sums), HEAD, 1)
    in_other = flip(after(in_rows, late_other), HEAD, 1)
    mixed, mixer_grad, gate_low, state_add, leaving, gain_sum = call(
        functools.partial(gate_kernel, width, inner_total),
        ins=[
            (BLOCK, mixer),
            (BLOCK, gate_pre),
            (BLOCK, mixed_grad),
            (BLOCK, act),
            (BLOCK, cum),
            (PLACE, sums),
            (ALL, gain),
        ],
        outs=[
            (BLOCK, inner, BF16),
            (BLOCK, inner, F32),
            (BLOCK, inner, BF16),
            (PLACE, states, F32),
            (SEQ, message, F32),
            (ALL, (8, cols), F32),
        ],
        scratch=[((cols, state), F32), ((8, LANES), F32)],
        reverse=True,
        load=(10, 14),
        near=(0, 1, 2, 3, 4),
    )
    came = [shift(leaving, PLANE, -1)]
    mixed_got = to_other_core([mixed])
    deep = WAYS * rows

    group = LANES // math.gcd(deep, LANES)

    def tile(value):
        return (value, (blocks, block_len, group * deep), lambda i: (0, 0, i))

    (early_w,) = plain_call(
        early_grad_kernel,
        (planes // group,),
        [tile(tokens), whole(gate_low), tile(cot_low), whole(mixed)],
        [((planes, 2 * cols, deep), BF16, (group, 2 * cols, deep), lambda i: (i, 0, 0))],
        (9, 24),
        scratch=[((2 * cols, blocks * block_len), BF16)],
    )
    came.append(shift(after(came[0], early_w), PLANE, -1))
    out_merged = join_matmul(
        [mixed], after(mixed_got, came[0]), [late_rows], [late_other], [(cols, cols)], None, (6, 24), (3,), ()
    )
    came.append(shift(after(came[1], out_merged), PLANE, -1))
    for _ in range(4, planes):
        came.append(shift(came[-1], PLANE, -1))
    early_rows = lax.psum_scatter(
        after(early_w, came), PLANE, scatter_dimension=0, tiled=True
    )
    gate_got = to_other_core([gate_low])
    mixer_grad = after(mixer_grad, (out_merged[2:], in_other))
    chan_low, edge, first_rows, taps_sum = call(
        functools.partial(back_kernel, width),
        ins=[
            (BLOCK, act),
            (BLOCK, conv),
            (BLOCK, pre),
            (BLOCK, cum),
            (BLOCK, cum_t),
            (BLOCK, step_size),
            (BLOCK, step_slope),
            (BLOCK, mixer_grad),
            (PLACE, incoming),
            (PLACE, state_add),
            (SEQ, halo),
            (ALL, taps_all),
            (ALL, rate),
            (ALL, skip),
        ]
        + [(SEQ, v) for v in came],
        outs=[
            (BLOCK, (blocks, block_len, first), BF16),
            (SEQ, (num_seqs, EDGE, mixed_cols), F32),
            (SEQ, (num_seqs, 8, mixed_cols), F32),
            (ALL, (8, mixed_cols), F32),
        ],
        scratch=[
            ((cols, state), F32),
            ((block_len + 8, mixed_cols), F32),
        ],
        reverse=True,
        load=(28, 22),
        near_outs=(0,),
    )
    following = shift(first_rows, PLANE, -1)
    late = jnp.concatenate([jnp.zeros_like(edge), following], axis=1)
    fix = sum(taps_all[k] * late[:, taps - 1 - k : taps - 1 - k + EDGE] for k in range(taps))
    fixed = after((edge + fix).astype(BF16), early_rows)
    for s in range(num_seqs):
        chan_low = lax.dynamic_update_slice(
            chan_low, fixed[s : s + 1], (order[s * WAYS + WAYS - 1], block_len - EDGE, 0)
        )
    out_parts, out_sent = plane_middle(out_merged, chan_low, (2, 14))
    part_at = part.astype(jnp.int32)[None]

    def exchanged(pieces):
        return [pieces[0]] + [flip(pieces[k], PART, k) for k in range(1, WAYS)]

    chan_low, out_sent, gate_got = lax.optimization_barrier((chan_low, out_sent, gate_got))
    low_got = gate_got + to_other_core([chan_low])
    out_mine = plane_sum(out_parts, out_sent)

    inner_w, state_w, state_other, step_w = plain_call(
        late_grad_kernel,
        (planes // group,),
        [tile(tokens), whole(chan_low)],
        [
            ((planes, c, deep), dtype, (group, c, deep), lambda i: (i, 0, 0))
            for c, dtype in ((cols, BF16), (state, F32), (state, F32), (EDGE, BF16))
        ],
        (9, 22),
        near=(1,),
        scalars=(core_at,),
        scratch=[((first, blocks * block_len), BF16)],
    )
    arrived = flip(state_other, HEAD, 1)
    plane_at = plane.astype(jnp.int32)[None]
    tall = cols + state + EDGE

    def crossed(value):
        block = (1,) + value.shape[1:]
        return pl.BlockSpec(block, lambda k, p: (p[0] ^ k, 0, 0))

    def flat_out(dtype):
        return result((tall, deep), dtype, False)

    own_chunk, *sent_chunks = pl.pallas_call(
        chunk_kernel,
        grid_spec=pltpu.PrefetchScalarGridSpec(
            num_scalar_prefetch=1,
            grid=(planes,),
            in_specs=[crossed(v) for v in (inner_w, state_w, arrived, step_w)],
            out_specs=[pl.BlockSpec((tall, deep), lambda k, p: (0, 0))] * planes,
        ),
        out_shape=[flat_out(F32)] + [flat_out(BF16)] * (planes - 1),
        compiler_params=pltpu.CompilerParams(
            dimension_semantics=("arbitrary",), vmem_limit_bytes=8 * MIB
        ),
        cost_estimate=cost_of(3),
    )(plane_at, *[pinned(v, False) for v in (inner_w, state_w, arrived, step_w)])
    got_chunks = [flip(v, PLANE, k + 1) for k, v in enumerate(sent_chunks)]
    *normed_merged, gain_local = join_matmul(
        [after(gate_low, own_chunk), chan_low],
        low_got,
        [late_rows, in_rows],
        [late_other, in_other],
        [(0, cols), (0, first)],
        tokens,
        (11, 30),
        (1, 2, 3, 6, 7),
        (0, 1, 2, 3),
    )
    output = pair_add(core_at, out_mine, hidden, (4, 14))
    keep_a, keep_b, send_a, send_b = normed_merged
    send_a, send_b = after((send_a, send_b), got_chunks[0::2])
    normed_merged = (keep_a, keep_b, send_a, send_b)
    wide_pad = ((0, 0), (0, mixed_cols - cols))
    vector = jnp.concatenate([taps_sum, jnp.pad(gain_sum, wide_pad), jnp.pad(gain_local, wide_pad)])
    normed_parts, normed_sent = plane_middle(
        normed_merged, (got_chunks[1::2], output), (2, 14)
    )
    vector = total(vector, (PLANE,))
    line = 2 * cols + tall + state
    extra = -(-vector.shape[0] // EDGE) * EDGE
    late_pieces = plain_call(
        functools.partial(turn_kernel, cols, state),
        (1,),
        [whole(v) for v in [vector, early_rows[0], own_chunk] + got_chunks],
        [((rows + extra, line), BF16, None, None)] * WAYS,
        (3, 18),
        scalars=(part_at,),
        scratch=[((deep, line), F32)],
    )
    normed_parts = after(normed_parts, late_pieces)
    normed_grad = plane_sum(normed_parts, normed_sent)
    unit_mine = take(unit_rows, core)
    unit_grad = normed_grad * norm_gain
    hidden_mine = take(inv_rms, core) * (
        unit_grad - unit_mine * jnp.mean(unit_grad * unit_mine, axis=-1, keepdims=True)
    )
    hidden_grad = pair_add(core_at, hidden_mine, cotangent, (4, 14))
    late_got = exchanged([*late_pieces[:-1], after(late_pieces[-1], hidden_grad)])
    lines = 2 * (taps + 1) + model_width // state + 2
    sizes = (
        (rows, WAYS * cols),
        (rows, WAYS * cols),
        (rows, WAYS * cols),
        (rows + lines, state),
        (rows, WAYS * heads),
        (taps, WAYS * cols),
        (1, WAYS * cols),
        (1, WAYS * cols),
        (WAYS, 3 * LANES),
    )
    placed = plain_call(
        functools.partial(place_kernel, mixed_cols),
        (1,),
        [whole(v) for v in late_got],
        [(shape, F32, None, None) for shape in sizes],
        (4, 20),
        scalars=(part_at,),
    )
    gate_weight_grad, out_weight_grad, inner_weight_grad, final, step_weight_grad = placed[:5]
    conv_weight_grad, conv_bias_grad, out_gain_grad, by_head = placed[5:]
    other = flip(final, HEAD, 1)
    mine_first = core == 0
    state_weight_grad = jnp.concatenate(
        [
            jnp.where(mine_first, final[:rows], other[:rows]),
            jnp.where(mine_first, other[:rows], final[:rows]),
        ],
        axis=1,
    )
    shared = final[rows:] + other[rows:]
    state_conv = shared[: 2 * (taps + 1)].reshape(taps + 1, 2 * state)
    norm_gain_grad = shared[2 * (taps + 1) : lines - 2].reshape(-1) / norm_gain
    conv_bias_grad = conv_bias_grad[0]
    out_gain_grad = out_gain_grad[0]
    by_head = by_head.reshape(WAYS, 3, LANES)[:, :, :heads]
    step_bias_grad, log_rate_grad, skip_gain_grad = [by_head[:, i].reshape(-1) for i in range(3)]
    return (
        output,
        hidden_grad,
        norm_gain_grad,
        gate_weight_grad,
        inner_weight_grad,
        state_weight_grad,
        step_weight_grad,
        conv_weight_grad,
        conv_bias_grad,
        state_conv[:taps],
        state_conv[taps],
        step_bias_grad,
        log_rate_grad,
        skip_gain_grad,
        out_gain_grad,
        out_weight_grad,
    )


def solution(mesh):
    grid = mesh.devices
    fine = Mesh(
        grid.reshape(grid.shape[0] // WAYS, WAYS, grid.shape[1]), (PLANE, PART, HEAD)
    )
    seq = (PLANE, PART)
    tokens, table, columns = P(None, seq, None), P(seq, HEAD), P(HEAD)
    return jax.shard_map(
        per_device,
        mesh=fine,
        in_specs=(
            tokens,
            P(),
            table,
            table,
            P(seq, None),
            table,
            P(None, HEAD),
            columns,
            P(),
            P(),
            columns,
            columns,
            columns,
            columns,
            table,
            tokens,
        ),
        out_specs=(
            tokens,
            tokens,
            P(),
            table,
            table,
            P(seq, None),
            table,
            P(None, HEAD),
            columns,
            P(),
            P(),
            columns,
            columns,
            columns,
            columns,
            table,
        ),
        check_vma=False,
    )
```
